256 devices in a mesh: rep: 4 (over x), node: 8 (over z), local: 8 (over y, core).
Axes of the slice: x: 4, y: 4, z: 8, core: 2. Of those that a mesh axis runs over, the one named last changes fastest.
Arguments:
- tokens: bfloat16 [32768, 3584], P(('rep', 'node', 'local')), may hold values from -6 to 6
- grad_out: bfloat16 [32768, 3584], P(('rep', 'node', 'local')), may hold values from -6 to 6
- gates: float32 [32768, 1], P(('rep', 'node', 'local')), may hold values from 0.2 to 1
- routes: int32 [32768, 1], P(('rep', 'node', 'local')), may hold values from 0 to 15; in each aligned block of 128 rows (0 to 127, 128 to 255, ...) at most 12 rows name the same one
- w_gate: bfloat16 [64, 3584, 256], P(('node', 'local')), may hold values from -0.09375 to 0.09375
- w_up: bfloat16 [64, 3584, 256], P(('node', 'local')), may hold values from -0.09375 to 0.09375
- w_down: bfloat16 [64, 256, 3584], P(('node', 'local')), may hold values from -0.1875 to 0.1875
Outputs:
- grad_tokens: bfloat16 [32768, 3584], P(('rep', 'node', 'local'))
- grad_gate: bfloat16 [64, 3584, 256], P(('node', 'local'), 'rep')
- grad_up: bfloat16 [64, 3584, 256], P(('node', 'local'), 'rep')
- grad_down: bfloat16 [64, 256, 3584], P(('node', 'local'), None, 'rep')
The draws below stay inside these ranges and needn't reach their ends.
Inputs may be any that keep to these rules, and one draw needn't show every extreme that they name: Among the 128 tokens of one device, no expert is named by more than 12 routes; in some such block an expert is named by exactly 12.
All inputs are finite; a program needn't handle non-finite values.
Results may differ from the reference program's by a relative error of at most 0.013.
Values may be sent and summed in bfloat16 or wider, within the bound.
A program may use at most 128 MiB of HBM per device.

```python
import math
import jax
import jax.numpy as jnp
import numpy as np
from jax import lax

D = 3584
FF = 1024
TOPK = 1
TOK_DEV = 128
HSPLIT = 4
EXPERTS = 16
SLOT = 12
TOKENS = 32768
N_REP = 4
N_NODE = 8
N_LOCAL = 8


def steps_of(rng, dims, pieces, low, largest):
    factor_of, own = 1.0, jax.random.fold_in(rng, 6)
    for position, parts in pieces:
        draws = jnp.exp(jax.random.uniform(jax.random.fold_in(own, position), (parts,), jnp.float32, low / len(pieces), largest / len(pieces)))
        factor_of = factor_of * jnp.repeat(draws, dims[position] // parts).reshape([-1 if axis == position else 1 for axis in range(len(dims))])
    return factor_of


def assign_block(rng, own, number, rows, amount, top, bound, skew):
    order = jax.random.permutation(rng, amount)
    packed, ordinary = shares(amount, rows * top, bound, skew, True), shares(amount, rows * top, bound, skew, False)
    places = jnp.arange(amount)

    def named(tallies, turn):
        used = int((tallies > 0).sum())
        fixed = max(1, used // 4)
        passed = fixed + (places - fixed + turn * (used - fixed)) % max(1, amount - fixed)
        return jnp.zeros((amount,), jnp.int32).at[order[jnp.where(places < fixed, places, passed)]].set(jnp.asarray(tallies, jnp.int32))

    tallies = jnp.where(number % 4 == 0, named(packed, number // 4), named(ordinary, number - number // 4 - 1))
    mixed = jax.random.permutation(jax.random.fold_in(own, 3), amount)
    giver, sink = mixed[0:amount // 2 * 2:2], mixed[1:amount // 2 * 2:2]
    margin = jnp.minimum(tallies[giver] - 1, bound - tallies[sink]) // 2
    margin = jnp.where((giver == order[0]) | (sink == order[0]) | (tallies[sink] == 0), 0, jnp.maximum(margin, 0))
    passed = jax.random.randint(jax.random.fold_in(own, 4), (amount // 2,), 0, 1 << 20) % (margin + 1)
    tallies = tallies.at[giver].add(-passed).at[sink].add(passed)
    labels = jnp.searchsorted(jnp.cumsum(tallies), jnp.arange(rows * top), side="right").astype(jnp.int32)
    grid = labels.reshape(top, rows).T
    grid = grid[jax.random.permutation(jax.random.fold_in(own, 1), rows)]
    turn = jax.random.randint(jax.random.fold_in(own, 2), (rows, 1), 0, top)
    return jnp.take_along_axis(grid, (jnp.arange(top)[None, :] + turn) % top, axis=1)


def shares(count, total, most, skew, full):
    portions = [(1 << 20) // math.isqrt(grade ** skew) + 1 for grade in range(1, count + 1)]
    largest = most if full else min(most, max(-(-total // count), total * portions[0] // sum(portions)))
    least = 1 if total - largest >= count - 1 else 0
    counts, spare = [largest] + [least] * (count - 1), total - largest - least * (count - 1)
    while spare > 0:
        free = [i for i in range(1, count) if counts[i] < largest] or [i for i in range(1, count) if counts[i] < most]
        pool, budget = sum([portions[i] for i in free]), spare
        for i in free:
            more = min(most - counts[i], max(1, budget * portions[i] // pool), spare)
            counts[i] = counts[i] + more
            spare = spare - more
    return np.array(counts)


def normal_values(rng, dims, width, reach, shards=(), kind=jnp.bfloat16):
    values = width * jax.random.normal(rng, dims, jnp.float32)
    if shards:
        values = values * steps_of(rng, dims, shards, -0.22, 0.18)
    return jnp.clip(values, -reach, reach).astype(kind)


def setup_inputs(seed: int = 0) -> dict:
    key_of = jax.random.split(jax.random.key(seed), 8)
    tokens = normal_values(key_of[0], (TOKENS, D), 1.0, 6.0, ((0, 256),))
    grad_out = normal_values(key_of[1], (TOKENS, D), 1.0, 6.0, ((0, 256),))
    gates = jnp.clip(0.2 + 0.8 * jax.random.uniform(key_of[2], (TOKENS, TOPK), jnp.float32) ** steps_of(key_of[2], (TOKENS, TOPK), ((0, 256),), -0.2, 0.2), 0.2, 1.0)
    routes_keys = jax.random.split(jax.random.fold_in(key_of[3], 1), TOKENS // TOK_DEV)
    routes_turns = jax.random.permutation(jax.random.fold_in(key_of[3], 3), TOKENS // TOK_DEV)
    routes = jax.vmap(lambda own, number: assign_block(jax.random.fold_in(key_of[3], 2), own, number, TOK_DEV, EXPERTS, TOPK, SLOT, 2))(routes_keys, routes_turns).reshape((TOKENS, TOPK))
    w_gate = normal_values(key_of[4], (EXPERTS * HSPLIT, D, FF // HSPLIT), D ** -0.5, 0.09375, ((0, 64),))
    w_up = normal_values(key_of[5], (EXPERTS * HSPLIT, D, FF // HSPLIT), D ** -0.5, 0.09375, ((0, 64),))
    w_down = normal_values(key_of[6], (EXPERTS * HSPLIT, FF // HSPLIT, D), FF ** -0.5, 0.1875, ((0, 64),))
    return dict(tokens=tokens, grad_out=grad_out, gates=gates, routes=routes, w_gate=w_gate, w_up=w_up, w_down=w_down)


def reference(tokens, grad_out, gates, routes, w_gate, w_up, w_down):
    hidden_part = FF // HSPLIT
    group = N_NODE * N_LOCAL
    rep_tokens = TOK_DEV * group
    route_count = rep_tokens * TOPK
    capacity = group * SLOT
    full_gate = w_gate.reshape(EXPERTS, HSPLIT, D, hidden_part).transpose(0, 2, 1, 3).reshape(EXPERTS, D, FF)
    full_up = w_up.reshape(EXPERTS, HSPLIT, D, hidden_part).transpose(0, 2, 1, 3).reshape(EXPERTS, D, FF)
    full_down = w_down.reshape(EXPERTS, FF, D)
    expert_ids = routes.reshape(N_REP, route_count)
    gate_values = gates.reshape(N_REP, route_count)
    rep_rows = tokens.reshape(N_REP, rep_tokens, D)
    rep_grads = grad_out.reshape(N_REP, rep_tokens, D)

    def one_expert(carry, expert):
        gate_mat = full_gate[expert]
        up_mat = full_up[expert]
        down_mat = full_down[expert]
        sum_gate = jnp.zeros((D, FF), jnp.float32)
        sum_up = jnp.zeros((D, FF), jnp.float32)
        sum_down = jnp.zeros((FF, D), jnp.float32)
        updated = []
        for replica in range(N_REP):
            chosen = expert_ids[replica] == expert
            order = jnp.argsort(jnp.where(chosen, 0, 1).astype(jnp.int32), stable=True).astype(jnp.int32)[:capacity]
            count = jnp.sum(chosen.astype(jnp.int32))
            valid = jnp.arange(capacity, dtype=jnp.int32) < count
            token_index = order // TOPK
            inputs = jnp.where(valid[:, None], rep_rows[replica][token_index], jnp.zeros((), jnp.bfloat16)).astype(jnp.bfloat16)
            upstream = jnp.where(valid[:, None], gate_values[replica][order][:, None] * rep_grads[replica][token_index].astype(jnp.float32), 0.0).astype(jnp.bfloat16)
            pre_gate = jnp.dot(inputs, gate_mat, preferred_element_type=jnp.float32)
            pre_up = jnp.dot(inputs, up_mat, preferred_element_type=jnp.float32)
            sigma = jax.nn.sigmoid(pre_gate)
            hidden = (pre_gate * sigma * pre_up).astype(jnp.bfloat16)
            grad_hidden = jnp.dot(upstream, down_mat.T, preferred_element_type=jnp.float32)
            grad_pre_gate = (grad_hidden * pre_up * sigma * (1.0 + pre_gate * (1.0 - sigma))).astype(jnp.bfloat16)
            grad_pre_up = (grad_hidden * pre_gate * sigma).astype(jnp.bfloat16)
            route_grad = (jnp.dot(grad_pre_gate, gate_mat.T, preferred_element_type=jnp.float32)
                          + jnp.dot(grad_pre_up, up_mat.T, preferred_element_type=jnp.float32)).astype(jnp.bfloat16)
            target = jnp.where(valid, order, route_count).astype(jnp.int32)
            updated.append(carry[replica].at[target].set(route_grad, mode="drop"))
            sum_gate = sum_gate + jnp.dot(inputs.T, grad_pre_gate, preferred_element_type=jnp.float32).astype(jnp.bfloat16).astype(jnp.float32)
            sum_up = sum_up + jnp.dot(inputs.T, grad_pre_up, preferred_element_type=jnp.float32).astype(jnp.bfloat16).astype(jnp.float32)
            sum_down = sum_down + jnp.dot(hidden.T, upstream, preferred_element_type=jnp.float32).astype(jnp.bfloat16).astype(jnp.float32)
        return tuple(updated), (sum_gate.astype(jnp.bfloat16), sum_up.astype(jnp.bfloat16), sum_down.astype(jnp.bfloat16))

    start = tuple(jnp.zeros((route_count, D), jnp.bfloat16) for replica in range(N_REP))
    finished, stacked = lax.scan(one_expert, start, jnp.arange(EXPERTS, dtype=jnp.int32))
    all_routes = jnp.stack(finished).reshape(TOKENS, TOPK, D)
    grad_tokens = jnp.sum(all_routes.astype(jnp.float32), axis=1).astype(jnp.bfloat16)
    grad_gate = stacked[0].reshape(EXPERTS, D, HSPLIT, hidden_part).transpose(0, 2, 1, 3).reshape(EXPERTS * HSPLIT, D, hidden_part)
    grad_up = stacked[1].reshape(EXPERTS, D, HSPLIT, hidden_part).transpose(0, 2, 1, 3).reshape(EXPERTS * HSPLIT, D, hidden_part)
    grad_down = stacked[2].reshape(EXPERTS * HSPLIT, hidden_part, D)
    return (grad_tokens, grad_gate, grad_up, grad_down)
```

```python
import jax
import jax.numpy as jnp
from jax import lax
from jax.experimental import pallas as pl
from jax.experimental.pallas import tpu as pltpu
from jax.sharding import PartitionSpec as P

MESH = pl.DeviceIdType.MESH
BF = jnp.bfloat16
F32 = jnp.float32

D = 3584
HALF = D // 2
QUART = D // 4
F = 256
T = 128
NZ = 8
SLOT = 24
UNIT = 2 * SLOT
NT_ROWS = (((1,), (1,)), ((), ()))


def offset_of(k):
    return ((k + 1) // 2) * (1 - 2 * ((k + 1) % 2))


def kernel(
    tok_hbm, grad_hbm, gate_ref, route_ref, wg_hbm, wu_hbm, wd_hbm,
    gt_ref, gw_ref,
    stage, meta, out, x, wg, wu, wd, gp, at, part, rda, rdb, ry, ret, w, ar, br, fin_send, fin_recv, place,
    loc, ex_s, ex_r, z_s, z_r, y_s, y_r, d1_s, d1_r, d2_s, d2_r,
    ra_s, ra_r, rb_s, rb_r, ryy_s, ryy_r, h_s, h_r, rs_s, rs_r, f_s, f_r,
):
    r = lax.axis_index("rep")
    z = lax.axis_index("node")
    l = lax.axis_index("local")
    y = l // 2
    c = l % 2
    pair = y // 2
    core_peer = (r, z, y * 2 + 1 - c)
    y_peer = (r, z, (y + 1 - 2 * (y % 2)) * 2 + c)
    x_next = ((r + 1) % 4, z, l)
    x_prev = ((r + 3) % 4, z, l)
    same = 1 - (pair + c) % 2
    far = 3 - y
    dest_l = same * (y * 2 + 1 - c) + (1 - same) * (far * 2 + c)
    src_l = (1 - same) * (y * 2 + pair) + same * (far * 2 + pair)

    def dest(k):
        return (r, (z + offset_of(k) + NZ) % NZ, dest_l)

    def source(k):
        return (r, (z - offset_of(k) + NZ) % NZ, src_l)

    def rcopy(src, dst, s, q, dev):
        return pltpu.make_async_remote_copy(
            src_ref=src, dst_ref=dst, send_sem=s, recv_sem=q, device_id=dev, device_id_type=MESH
        )

    mine = pl.ds(pl.multiple_of(c * T, T), T)
    mine_g = pl.ds(pl.multiple_of(2 * T + c * T, T), T)
    local = [
        pltpu.make_async_copy(tok_hbm, stage.at[mine], loc.at[0]),
        pltpu.make_async_copy(grad_hbm, stage.at[mine_g], loc.at[1]),
        pltpu.make_async_copy(wg_hbm, wg, loc.at[2]),
        pltpu.make_async_copy(wu_hbm, wu, loc.at[3]),
        pltpu.make_async_copy(wd_hbm, wd, loc.at[4]),
    ]
    for copy in local:
        copy.start()
    row8 = lax.broadcasted_iota(jnp.int32, (8, T), 0)
    meta[c] = jnp.where(row8 == 0, route_ref[...].astype(F32), gate_ref[...])

    barrier = pltpu.get_barrier_semaphore()
    for dev in (core_peer, y_peer, x_next, x_prev):
        pl.semaphore_signal(barrier, inc=1, device_id=dev, device_id_type=MESH)

    def greet(k, carry):
        pl.semaphore_signal(barrier, inc=1, device_id=dest(k), device_id_type=MESH)
        pl.semaphore_signal(barrier, inc=1, device_id=source(k), device_id_type=MESH)
        return carry

    lax.fori_loop(0, NZ, greet, 0)
    pl.semaphore_wait(barrier, 4 + 2 * NZ)

    exchange = [
        rcopy(meta.at[c], meta.at[c], ex_s.at[0], ex_r.at[0], core_peer),
        rcopy(tok_hbm, stage.at[mine], ex_s.at[1], ex_r.at[1], core_peer),
        rcopy(grad_hbm, stage.at[mine_g], ex_s.at[2], ex_r.at[2], core_peer),
    ]
    for copy in exchange:
        copy.start()
    exchange[0].wait_recv()
    route = jnp.concatenate([meta[0, 0:1, :], meta[1, 0:1, :]], axis=1)
    gate = jnp.concatenate([meta[0, 1:2, :], meta[1, 1:2, :]], axis=1)
    expert = lax.broadcasted_iota(jnp.int32, (16, 2 * T), 0)
    wanted = jnp.where(expert < NZ, 2 * expert + c, -1).astype(F32)
    match = jnp.where(route == wanted, 1.0, 0.0)
    earlier = lax.broadcasted_iota(jnp.int32, (2 * T, 2 * T), 0) < lax.broadcasted_iota(
        jnp.int32, (2 * T, 2 * T), 1
    )
    before = jnp.dot(
        match.astype(BF), jnp.where(earlier, 1.0, 0.0).astype(BF), preferred_element_type=F32
    )
    position = jnp.sum(before * match, axis=0, keepdims=True)
    number = jnp.sum(expert.astype(F32) * match, axis=0, keepdims=True)
    known = jnp.sum(match, axis=0, keepdims=True) > 0.5
    target = jnp.where(known, number * SLOT + position, -1.0)
    place[...] = jnp.broadcast_to(jnp.where(known, number * UNIT + position, -1000.0), (8, 2 * T))
    slots = lax.broadcasted_iota(jnp.int32, (NZ * SLOT, 2 * T), 0).astype(F32)
    chosen = slots == target
    slot_gate = jnp.sum(jnp.where(chosen, gate, 0.0), axis=1, keepdims=True)
    pick = jnp.where(chosen, 1.0, 0.0).astype(BF)
    local[0].wait()
    local[1].wait()
    exchange[1].wait_recv()
    exchange[2].wait_recv()

    def pack(i, carry):
        cols = pl.ds(pl.multiple_of(i * 512, 512), 512)
        rows = jnp.dot(pick, stage[0 : 2 * T, cols], preferred_element_type=F32)
        ups = jnp.dot(pick, stage[2 * T : 4 * T, cols], preferred_element_type=F32) * slot_gate
        both = jnp.concatenate(
            [rows.reshape(NZ, SLOT, 512), ups.reshape(NZ, SLOT, 512)], axis=1
        )
        out[:, :, cols] = both.astype(BF)
        return carry

    lax.fori_loop(0, D // 512, pack, 0)

    def send_unit(k):
        return rcopy(
            out.at[(z + offset_of(k) + NZ) % NZ], x.at[k, 0], z_s.at[k], z_r.at[k], dest(k)
        )

    def fwd_y(k):
        return rcopy(x.at[k, 0], x.at[k, 2], y_s.at[k], y_r.at[k], y_peer)

    def fwd_d1(k):
        return rcopy(x.at[k, 0], x.at[k, 1], d1_s.at[k], d1_r.at[k], core_peer)

    def fwd_d2(k):
        return rcopy(x.at[k, 2], x.at[k, 3], d2_s.at[k], d2_r.at[k], core_peer)

    def send_one(k, carry):
        send_unit(k).start()
        return carry

    lax.fori_loop(0, NZ, send_one, 0)
    for copy in local[2:]:
        copy.wait()

    def forward_group(g):
        units = x.at[pl.ds(2 * g, 2)]
        rows = units[...].reshape(8 * UNIT, D)
        pre_g = jnp.dot(rows, wg[...], preferred_element_type=F32)
        pre_u = jnp.dot(rows, wu[...], preferred_element_type=F32)
        gh = lax.dot_general(rows, wd[...], NT_ROWS, preferred_element_type=F32)
        a = pre_g.reshape(8, UNIT, F)[:, :SLOT]
        u = pre_u.reshape(8, UNIT, F)[:, :SLOT]
        h = gh.reshape(8, UNIT, F)[:, SLOT:]
        sigma = 1.0 / (1.0 + jnp.exp(-a))
        swish = a * sigma
        hidden = swish * u
        d_gate = h * u * sigma * (1.0 + a * (1.0 - sigma))
        d_up = h * swish
        gp[pl.ds(pl.multiple_of(g * 192, 64), 192), 0:F] = d_gate.reshape(192, F).astype(BF)
        gp[pl.ds(pl.multiple_of(g * 192, 64), 192), F : 2 * F] = d_up.reshape(192, F).astype(BF)
        zero = jnp.zeros_like(a)
        cols = pl.ds(pl.multiple_of(g * 384, 128), 384)

        def put(first, rest, top):
            both = jnp.concatenate([first, rest], axis=1).reshape(8 * UNIT, F)
            at[top : top + F, cols] = both.T.astype(BF)

        put(d_gate, zero, 0)
        put(d_up, zero, F)
        put(zero, hidden, 2 * F)

    def send_ra(k):
        return rcopy(part.at[k, 1], rda.at[k], ra_s.at[k], ra_r.at[k], core_peer)

    def send_rb(k):
        return rcopy(part.at[k, 3], rdb.at[k], rb_s.at[k], rb_r.at[k], core_peer)

    def route_group(g):
        rows = pl.ds(pl.multiple_of(g * 192, 64), 192)
        left = gp[rows, 0:F]
        right = gp[rows, F : 2 * F]

        def columns(i, carry):
            done = []
            for half in range(2):
                cols = pl.ds(pl.multiple_of(half * HALF + i * 256, 256), 256)
                one = lax.dot_general(left, wg[cols, :], NT_ROWS, preferred_element_type=F32)
                one += lax.dot_general(right, wu[cols, :], NT_ROWS, preferred_element_type=F32)
                done.append(one.reshape(2, 4, SLOT, 256))
            part[pl.ds(2 * g, 2), :, :, pl.ds(pl.multiple_of(i * 256, 256), 256)] = (
                jnp.concatenate(done, axis=2).astype(BF)
            )
            return carry

        lax.fori_loop(0, HALF // 256, columns, 0)
        for kk in range(2):
            send_ra(2 * g + kk).start()
            send_rb(2 * g + kk).start()

    def turn(i, carry):
        @pl.when(i < 4)
        def _():
            for kk in range(2):
                k = 2 * i + kk
                send_unit(k).wait_recv()
                fwd_y(k).start()
                fwd_d1(k).start()

        @pl.when(i > 0)
        def _():
            for kk in range(2):
                k = 2 * i - 2 + kk
                fwd_y(k).wait_recv()
                fwd_d2(k).start()
            for kk in range(2):
                k = 2 * i - 2 + kk
                fwd_d1(k).wait_recv()
                fwd_d2(k).wait_recv()
            forward_group(i - 1)

        @pl.when((i > 0) & (i < 4))
        def _():
            route_group(i - 1)

        return carry

    lax.fori_loop(0, 5, turn, 0)

    def weight_chunk(q):
        cols = pl.ds(pl.multiple_of(q * QUART, 128), QUART)
        rows = x[:, :, :, cols].reshape(32 * UNIT, QUART)

        def block(m, carry):
            these = pl.ds(pl.multiple_of(m * 256, 256), 256)
            w[q, these, :] = jnp.dot(at[these, :], rows, preferred_element_type=F32).astype(BF)
            return carry

        lax.fori_loop(0, 3, block, 0)

    opposite, nxt, prv = (r + 2) % 4, (r + 1) % 4, (r + 3) % 4
    low, high = pl.ds(0, 384), pl.ds(384, 384)
    reduce = [
        rcopy(w.at[opposite, low], ar.at[0], rs_s.at[0], rs_r.at[0], x_next),
        rcopy(w.at[opposite, high], ar.at[1], rs_s.at[1], rs_r.at[1], x_prev),
        rcopy(w.at[nxt, high], br.at[0, high], rs_s.at[2], rs_r.at[2], x_next),
        rcopy(w.at[prv, low], br.at[1, low], rs_s.at[3], rs_r.at[3], x_prev),
        rcopy(w.at[nxt, low], br.at[0, low], rs_s.at[4], rs_r.at[4], x_next),
        rcopy(w.at[prv, high], br.at[1, high], rs_s.at[5], rs_r.at[5], x_prev),
    ]

    def step(j, carry):
        weight_chunk((r + 2 + j + (j // 2)) % 4)

        @pl.when(j == 0)
        def _():
            reduce[0].start()
            reduce[1].start()

        @pl.when(j == 1)
        def _():
            reduce[3].start()

        @pl.when(j == 2)
        def _():
            reduce[2].start()

        @pl.when(j == 2)
        def _():
            route_group(3)

        return carry

    lax.fori_loop(0, 3, step, 0)

    def across(k, carry):
        send_rb(k).wait_recv()
        part[k, 2] = (part[k, 2].astype(F32) + rdb[k].astype(F32)).astype(BF)
        rcopy(part.at[k, 2], ry.at[k], ryy_s.at[k], ryy_r.at[k], y_peer).start()
        return carry

    lax.fori_loop(0, NZ, across, 0)

    weight_chunk(r)

    reduce[0].wait_recv()
    w[nxt, 0:384, :] = (w[nxt, 0:384, :].astype(F32) + ar[0].astype(F32)).astype(BF)
    reduce[4].start()
    reduce[1].wait_recv()
    w[prv, 384:768, :] = (w[prv, 384:768, :].astype(F32) + ar[1].astype(F32)).astype(BF)
    reduce[5].start()

    def send_home(k):
        return rcopy(part.at[k, 0], ret.at[z], h_s.at[k], h_r.at[z], source(k))

    def home(k, carry):
        send_ra(k).wait_recv()
        rcopy(part.at[k, 2], ry.at[k], ryy_s.at[k], ryy_r.at[k], y_peer).wait_recv()
        part[k, 0] = (
            part[k, 0].astype(F32) + rda[k].astype(F32) + ry[k].astype(F32)
        ).astype(BF)
        send_home(k).start()
        return carry

    lax.fori_loop(0, NZ, home, 0)

    def arrived(j, carry):
        rcopy(part.at[j, 0], ret.at[j], h_s.at[j], h_r.at[j], source(0)).wait_recv()
        return carry

    lax.fori_loop(0, NZ, arrived, 0)

    unit_rows = lax.broadcasted_iota(jnp.int32, (NZ * UNIT, 2 * T), 0).astype(F32)

    def last(i, carry):
        cols = pl.ds(pl.multiple_of(i * 256, 256), 256)
        rows = ret[:, :, cols].reshape(NZ * UNIT, 256)
        for half in range(2):
            pick_t = jnp.where(unit_rows == place[0:1, :] + half * SLOT, 1.0, 0.0).astype(BF)
            got = lax.dot_general(
                pick_t, rows, (((0,), (0,)), ((), ())), preferred_element_type=F32
            )
            both = got.reshape(2, T, 256).astype(BF)
            outc = pl.ds(pl.multiple_of(half * HALF + i * 256, 256), 256)
            fin_send[:, :, outc] = both
        return carry

    lax.fori_loop(0, HALF // 256, last, 0)
    final = rcopy(fin_send.at[1 - c], fin_recv, f_s, f_r, core_peer)
    final.start()
    final.wait_recv()
    gt_ref[...] = (fin_send[c].astype(F32) + fin_recv[...].astype(F32)).astype(BF)

    for j in (2, 3, 4, 5):
        reduce[j].wait_recv()
    gw_ref[...] = (
        w[r].astype(F32) + br[0].astype(F32) + br[1].astype(F32)
    ).astype(BF)

    for copy in exchange + reduce + [final]:
        copy.wait_send()

    def drain(k, carry):
        send_unit(k).wait_send()
        fwd_y(k).wait_send()
        fwd_d1(k).wait_send()
        fwd_d2(k).wait_send()
        send_ra(k).wait_send()
        send_rb(k).wait_send()
        rcopy(part.at[k, 2], ry.at[k], ryy_s.at[k], ryy_r.at[k], y_peer).wait_send()
        send_home(k).wait_send()
        return carry

    lax.fori_loop(0, NZ, drain, 0)


def on_device(tokens, grad_out, gates, routes, w_gate, w_up, w_down):
    dma = pltpu.SemaphoreType.DMA
    vmem = pl.BlockSpec(memory_space=pltpu.VMEM)
    anyspace = pl.BlockSpec(memory_space=pl.ANY)
    flops = 2 * 1536 * D * F * 7
    grad_tokens, grads = pl.pallas_call(
        kernel,
        out_shape=(
            jax.ShapeDtypeStruct((T, D), BF),
            jax.ShapeDtypeStruct((3 * F, QUART), BF),
        ),
        in_specs=[anyspace, anyspace, vmem, vmem, anyspace, anyspace, anyspace],
        out_specs=(vmem, vmem),
        scratch_shapes=[
            pltpu.VMEM((4 * T, D), BF),
            pltpu.VMEM((2, 8, T), F32),
            pltpu.VMEM((NZ, UNIT, D), BF),
            pltpu.VMEM((NZ, 4, UNIT, D), BF),
            pltpu.VMEM((D, F), BF),
            pltpu.VMEM((D, F), BF),
            pltpu.VMEM((F, D), BF),
            pltpu.VMEM((768, 2 * F), BF),
            pltpu.VMEM((3 * F, 32 * UNIT), BF),
            pltpu.VMEM((NZ, 4, UNIT, HALF), BF),
            pltpu.VMEM((NZ, UNIT, HALF), BF),
            pltpu.VMEM((NZ, UNIT, HALF), BF),
            pltpu.VMEM((NZ, UNIT, HALF), BF),
            pltpu.VMEM((NZ, UNIT, HALF), BF),
            pltpu.VMEM((4, 3 * F, QUART), BF),
            pltpu.VMEM((2, 384, QUART), BF),
            pltpu.VMEM((2, 3 * F, QUART), BF),
            pltpu.VMEM((2, T, D), BF),
            pltpu.VMEM((T, D), BF),
            pltpu.VMEM((8, 2 * T), F32),
            dma((5,)), dma((3,)), dma((3,)),
            dma((NZ,)), dma((NZ,)), dma((NZ,)), dma((NZ,)),
            dma((NZ,)), dma((NZ,)), dma((NZ,)), dma((NZ,)),
            dma((NZ,)), dma((NZ,)), dma((NZ,)), dma((NZ,)),
            dma((NZ,)), dma((NZ,)), dma((NZ,)), dma((NZ,)),
            dma((6,)), dma((6,)), dma, dma,
        ],
        compiler_params=pltpu.CompilerParams(
            collective_id=0, has_side_effects=True, vmem_limit_bytes=62 * 1024 * 1024
        ),
        cost_estimate=pl.CostEstimate(flops=flops, bytes_accessed=10_000_000, transcendentals=0),
    )(
        tokens, grad_out, gates.reshape(1, T), routes.reshape(1, T),
        w_gate[0], w_up[0], w_down[0],
    )
    return (
        grad_tokens,
        grads[:F].T[None],
        grads[F : 2 * F].T[None],
        grads[2 * F :][None],
    )


def solution(mesh):
    in_specs = (
        P(("rep", "node", "local"), None),
        P(("rep", "node", "local"), None),
        P(("rep", "node", "local"), None),
        P(("rep", "node", "local"), None),
        P(("node", "local"), None, None),
        P(("node", "local"), None, None),
        P(("node", "local"), None, None),
    )
    out_specs = (
        P(("rep", "node", "local"), None),
        P(("node", "local"), "rep", None),
        P(("node", "local"), "rep", None),
        P(("node", "local"), None, "rep"),
    )
    return jax.shard_map(
        on_device, mesh=mesh, in_specs=in_specs, out_specs=out_specs, check_vma=False
    )
```

```python
import jax
import jax.numpy as jnp
from jax import lax
from jax.experimental import pallas as pl
from jax.experimental.pallas import tpu as pltpu
from jax.sharding import PartitionSpec as P

MESH = pl.DeviceIdType.MESH
BF = jnp.bfloat16
F32 = jnp.float32

D = 3584
HALF = D // 2
QUART = D // 4
F = 256
T = 128
NZ = 8
SLOT = 24
UNIT = 2 * SLOT
NT_ROWS = (((1,), (1,)), ((), ()))


def offset_of(k):
    return ((k + 1) // 2) * (1 - 2 * ((k + 1) % 2))


def kernel(
    tok_hbm, grad_hbm, gate_ref, route_ref, wg_hbm, wu_hbm, wd_hbm,
    gt_ref, gw_ref,
    stage, meta, out, x, wg, wu, wd, at, part, rda, rdb, ry, ret, w, ar, br, fin_send, fin_recv, place,
    xt, xq, gall, acc,
    loc, ex_s, ex_r, z_s, z_r, y_s, y_r, d1_s, d1_r, d2_s, d2_r,
    ra_s, ra_r, rb_s, rb_r, ryy_s, ryy_r, h_s, h_r, rs_s, rs_r, f_s, f_r,
    xs_s, xs_r, xc_s, xc_r, gs_s, gs_r,
):
    r = lax.axis_index("rep")
    z = lax.axis_index("node")
    l = lax.axis_index("local")
    y = l // 2
    c = l % 2
    pair = y // 2
    core_peer = (r, z, y * 2 + 1 - c)
    y_peer = (r, z, (y + 1 - 2 * (y % 2)) * 2 + c)
    x_next = ((r + 1) % 4, z, l)
    x_prev = ((r + 3) % 4, z, l)
    x_far = ((r + 2) % 4, z, l)
    same = 1 - (pair + c) % 2
    far = 3 - y
    dest_l = same * (y * 2 + 1 - c) + (1 - same) * (far * 2 + c)
    src_l = (1 - same) * (y * 2 + pair) + same * (far * 2 + pair)

    def dest(k):
        return (r, (z + offset_of(k) + NZ) % NZ, dest_l)

    def source(k):
        return (r, (z - offset_of(k) + NZ) % NZ, src_l)

    def rcopy(src, dst, s, q, dev):
        return pltpu.make_async_remote_copy(
            src_ref=src, dst_ref=dst, send_sem=s, recv_sem=q, device_id=dev, device_id_type=MESH
        )

    mine = pl.ds(pl.multiple_of(c * T, T), T)
    mine_g = pl.ds(pl.multiple_of(2 * T + c * T, T), T)
    local = [
        pltpu.make_async_copy(tok_hbm, stage.at[mine], loc.at[0]),
        pltpu.make_async_copy(grad_hbm, stage.at[mine_g], loc.at[1]),
        pltpu.make_async_copy(wg_hbm, wg, loc.at[2]),
        pltpu.make_async_copy(wu_hbm, wu, loc.at[3]),
        pltpu.make_async_copy(wd_hbm, wd, loc.at[4]),
    ]
    for copy in local:
        copy.start()
    row8 = lax.broadcasted_iota(jnp.int32, (8, T), 0)
    meta[c] = jnp.where(row8 == 0, route_ref[...].astype(F32), gate_ref[...])

    barrier = pltpu.get_barrier_semaphore()
    for dev in (core_peer, y_peer, x_next, x_prev, x_far):
        pl.semaphore_signal(barrier, inc=1, device_id=dev, device_id_type=MESH)

    def greet(k, carry):
        pl.semaphore_signal(barrier, inc=1, device_id=dest(k), device_id_type=MESH)
        pl.semaphore_signal(barrier, inc=1, device_id=source(k), device_id_type=MESH)
        return carry

    lax.fori_loop(0, NZ, greet, 0)
    pl.semaphore_wait(barrier, 5 + 2 * NZ)

    exchange = [
        rcopy(meta.at[c], meta.at[c], ex_s.at[0], ex_r.at[0], core_peer),
        rcopy(tok_hbm, stage.at[mine], ex_s.at[1], ex_r.at[1], core_peer),
        rcopy(grad_hbm, stage.at[mine_g], ex_s.at[2], ex_r.at[2], core_peer),
    ]
    for copy in exchange:
        copy.start()
    exchange[0].wait_recv()
    route = jnp.concatenate([meta[0, 0:1, :], meta[1, 0:1, :]], axis=1)
    gate = jnp.concatenate([meta[0, 1:2, :], meta[1, 1:2, :]], axis=1)
    expert = lax.broadcasted_iota(jnp.int32, (16, 2 * T), 0)
    wanted = jnp.where(expert < NZ, 2 * expert + c, -1).astype(F32)
    match = jnp.where(route == wanted, 1.0, 0.0)
    earlier = lax.broadcasted_iota(jnp.int32, (2 * T, 2 * T), 0) < lax.broadcasted_iota(
        jnp.int32, (2 * T, 2 * T), 1
    )
    before = jnp.dot(
        match.astype(BF), jnp.where(earlier, 1.0, 0.0).astype(BF), preferred_element_type=F32
    )
    position = jnp.sum(before * match, axis=0, keepdims=True)
    number = jnp.sum(expert.astype(F32) * match, axis=0, keepdims=True)
    known = jnp.sum(match, axis=0, keepdims=True) > 0.5
    target = jnp.where(known, number * SLOT + position, -1.0)
    place[...] = jnp.broadcast_to(jnp.where(known, number * UNIT + position, -1000.0), (8, 2 * T))
    slots = lax.broadcasted_iota(jnp.int32, (NZ * SLOT, 2 * T), 0).astype(F32)
    chosen = slots == target
    slot_gate = jnp.sum(jnp.where(chosen, gate, 0.0), axis=1, keepdims=True)
    pick = jnp.where(chosen, 1.0, 0.0).astype(BF)
    local[0].wait()
    local[1].wait()
    exchange[1].wait_recv()
    exchange[2].wait_recv()

    def pack(i, carry):
        cols = pl.ds(pl.multiple_of(i * 512, 512), 512)
        rows = jnp.dot(pick, stage[0 : 2 * T, cols], preferred_element_type=F32)
        ups = jnp.dot(pick, stage[2 * T : 4 * T, cols], preferred_element_type=F32) * slot_gate
        both = jnp.concatenate(
            [rows.reshape(NZ, SLOT, 512), ups.reshape(NZ, SLOT, 512)], axis=1
        )
        out[:, :, cols] = both.astype(BF)
        return carry

    lax.fori_loop(0, D // 512, pack, 0)

    def send_unit(k):
        return rcopy(
            out.at[(z + offset_of(k) + NZ) % NZ], x.at[k, 0], z_s.at[k], z_r.at[k], dest(k)
        )

    def fwd_y(k):
        return rcopy(x.at[k, 0], x.at[k, 1], y_s.at[k], y_r.at[k], y_peer)

    def fwd_d1(k):
        return rcopy(x.at[k, 0], x.at[k, 2], d1_s.at[k], d1_r.at[k], core_peer)

    def fwd_d2(k):
        return rcopy(x.at[k, 1], x.at[k, 3], d2_s.at[k], d2_r.at[k], core_peer)

    def send_one(k, carry):
        send_unit(k).start()
        return carry

    lax.fori_loop(0, NZ, send_one, 0)
    for copy in local[2:]:
        copy.wait()

    def forward_group(g):
        units = x.at[pl.ds(2 * g, 2)]
        rows = units[...].reshape(8 * UNIT, D)
        pre_g = jnp.dot(rows, wg[...], preferred_element_type=F32)
        pre_u = jnp.dot(rows, wu[...], preferred_element_type=F32)
        gh = lax.dot_general(rows, wd[...], NT_ROWS, preferred_element_type=F32)
        a = pre_g.reshape(8, UNIT, F)[:, :SLOT]
        u = pre_u.reshape(8, UNIT, F)[:, :SLOT]
        h = gh.reshape(8, UNIT, F)[:, SLOT:]
        sigma = 1.0 / (1.0 + jnp.exp(-a))
        swish = a * sigma
        hidden = swish * u
        d_gate = h * u * sigma * (1.0 + a * (1.0 - sigma))
        d_up = h * swish
        gall[g, 0, :, 0:F] = d_gate.reshape(192, F).astype(BF)
        gall[g, 0, :, F : 2 * F] = d_up.reshape(192, F).astype(BF)
        cols = pl.ds(pl.multiple_of(g * 384, 128), 384)
        both = jnp.concatenate([jnp.zeros_like(hidden), hidden], axis=1).reshape(8 * UNIT, F)
        at[:, cols] = both.T.astype(BF)

    def quarter(q):
        return pl.ds(pl.multiple_of(q * QUART, 128), QUART)

    def xt_send(k, j):
        return rcopy(
            xt.at[k, :, quarter((r + j) % 4)], xq.at[k // 2, 4 - j, k % 2, 0],
            xs_s.at[k, j], xs_r.at[k, 4 - j], ((r + j) % 4, z, l),
        )

    def xt_got(k, j):
        return rcopy(
            xt.at[k, :, quarter(r)], xq.at[k // 2, j, k % 2, 0],
            xs_s.at[k, j], xs_r.at[k, j], ((r + j) % 4, z, l),
        )

    def xq_fwd(k, j):
        src = xt.at[k, :, quarter(r)] if j == 0 else xq.at[k // 2, j, k % 2, 0]
        return rcopy(src, xq.at[k // 2, j, k % 2, 1], xc_s.at[k, j], xc_r.at[k, j], core_peer)

    def g_send(g, j):
        return rcopy(
            gall.at[g, 0], gall.at[g, 4 - j], gs_s.at[g, j], gs_r.at[g, 4 - j], ((r + j) % 4, z, l)
        )

    def g_got(g, j):
        return rcopy(gall.at[g, 0], gall.at[g, j], gs_s.at[g, j], gs_r.at[g, j], ((r + j) % 4, z, l))

    def compact(k):
        def columns(i, carry):
            cols = pl.ds(pl.multiple_of(i * QUART, 128), QUART)
            both = x[k, 0:2, :, cols].astype(F32)[:, :SLOT]
            xt[k, :, cols] = both.reshape(UNIT, QUART).astype(BF)
            return carry

        lax.fori_loop(0, 4, columns, 0)
        xq[k // 2, 0, k % 2, 0] = xt[k, :, quarter(r)]
        for j in (2, 1, 3):
            xt_send(k, j).start()
        xq_fwd(k, 0).start()

    def relay_quarters(g):
        for kk in range(2):
            for j in (1, 2, 3):
                xt_got(2 * g + kk, j).wait_recv()
                xq_fwd(2 * g + kk, j).start()

    def send_grads(g):
        for j in (2, 1, 3):
            g_send(g, j).start()

    def accumulate(g, first):
        for kk in range(2):
            for j in range(4):
                xq_fwd(2 * g + kk, j).wait_recv()
        for j in (1, 2, 3):
            g_got(g, j).wait_recv()
        rows = xq[g].reshape(4 * 192, QUART)
        for m in range(2):
            left = gall[g, :, :, m * F : (m + 1) * F].reshape(4 * 192, F)
            term = lax.dot_general(left, rows, (((0,), (0,)), ((), ())), preferred_element_type=F32)
            if first:
                acc[m] = term
            else:
                acc[m] += term

    def send_ra(k):
        return rcopy(part.at[k, 2], rda.at[k], ra_s.at[k], ra_r.at[k], core_peer)

    def send_rb(k):
        return rcopy(part.at[k, 3], rdb.at[k], rb_s.at[k], rb_r.at[k], core_peer)

    def route_group(g):
        left = gall[g, 0, :, 0:F]
        right = gall[g, 0, :, F : 2 * F]

        def columns(i, carry):
            done = []
            for half in range(2):
                cols = pl.ds(pl.multiple_of(half * HALF + i * 256, 256), 256)
                one = lax.dot_general(left, wg[cols, :], NT_ROWS, preferred_element_type=F32)
                one += lax.dot_general(right, wu[cols, :], NT_ROWS, preferred_element_type=F32)
                done.append(one.reshape(2, 4, SLOT, 256))
            part[pl.ds(2 * g, 2), :, :, pl.ds(pl.multiple_of(i * 256, 256), 256)] = (
                jnp.concatenate(done, axis=2).astype(BF)
            )
            return carry

        lax.fori_loop(0, HALF // 256, columns, 0)
        for kk in range(2):
            send_ra(2 * g + kk).start()
            send_rb(2 * g + kk).start()

    def y_return(k):
        return rcopy(part.at[k, 1], ry.at[k], ryy_s.at[k], ryy_r.at[k], y_peer)

    def across(k):
        send_rb(k).wait_recv()
        part[k, 1] = (part[k, 1].astype(F32) + rdb[k].astype(F32)).astype(BF)
        y_return(k).start()

    def send_home(k):
        return rcopy(part.at[k, 0], ret.at[z], h_s.at[k], h_r.at[z], source(k))

    def home(k):
        send_ra(k).wait_recv()
        y_return(k).wait_recv()
        part[k, 0] = (
            part[k, 0].astype(F32) + rda[k].astype(F32) + ry[k].astype(F32)
        ).astype(BF)
        send_home(k).start()

    def turn(t, carry):
        @pl.when(t < NZ)
        def _():
            send_unit(t).wait_recv()
            fwd_y(t).start()
            fwd_d1(t).start()

        @pl.when(t > 0)
        def _():
            k = t - 1
            fwd_y(k).wait_recv()
            fwd_d2(k).start()
            compact(k)

        even = t % 2 == 0

        @pl.when(t == NZ)
        def _():
            def early(m, carry):
                across(5 - m)
                return carry

            lax.fori_loop(0, 6, early, 0)

        @pl.when((t > 0) & even)
        def _():
            for kk in range(2):
                fwd_d1(t - 2 + kk).wait_recv()
                fwd_d2(t - 2 + kk).wait_recv()
            forward_group(t // 2 - 1)

        @pl.when((t > 0) & (t < NZ) & even)
        def _():
            send_grads(t // 2 - 1)
            route_group(t // 2 - 1)

        @pl.when((t > 3) & even)
        def _():
            relay_quarters(t // 2 - 2)

        @pl.when(t == 6)
        def _():
            accumulate(0, True)

        @pl.when(t == 8)
        def _():
            accumulate(1, False)

        return carry

    lax.fori_loop(0, NZ + 1, turn, 0)

    def weight_chunk(q):
        rows = x[:, :, :, quarter(q)].reshape(32 * UNIT, QUART)
        w[q] = jnp.dot(at[...], rows, preferred_element_type=F32).astype(BF)

    opposite, nxt, prv = (r + 2) % 4, (r + 1) % 4, (r + 3) % 4
    low, high = pl.ds(0, 128), pl.ds(128, 128)
    reduce = [
        rcopy(w.at[opposite, low], ar.at[0], rs_s.at[0], rs_r.at[0], x_next),
        rcopy(w.at[opposite, high], ar.at[1], rs_s.at[1], rs_r.at[1], x_prev),
        rcopy(w.at[nxt, high], br.at[0, high], rs_s.at[2], rs_r.at[2], x_next),
        rcopy(w.at[prv, low], br.at[1, low], rs_s.at[3], rs_r.at[3], x_prev),
        rcopy(w.at[nxt, low], br.at[0, low], rs_s.at[4], rs_r.at[4], x_next),
        rcopy(w.at[prv, high], br.at[1, high], rs_s.at[5], rs_r.at[5], x_prev),
    ]

    def step(j, carry):
        weight_chunk((r + 2 + j + (j // 2)) % 4)

        @pl.when(j == 0)
        def _():
            reduce[0].start()
            reduce[1].start()
            send_grads(3)

        @pl.when(j == 1)
        def _():
            reduce[3].start()

        @pl.when(j == 2)
        def _():
            reduce[2].start()

        return carry

    lax.fori_loop(0, 3, step, 0)
    route_group(3)

    def late(m, carry):
        across(6 + m)
        return carry

    lax.fori_loop(0, 2, late, 0)

    def first_home(m, carry):
        home(5 - m)
        return carry

    lax.fori_loop(0, 3, first_home, 0)
    weight_chunk(r)
    relay_quarters(3)
    accumulate(2, False)

    reduce[0].wait_recv()
    w[nxt, 0:128, :] = (w[nxt, 0:128, :].astype(F32) + ar[0].astype(F32)).astype(BF)
    reduce[4].start()
    reduce[1].wait_recv()
    w[prv, 128:256, :] = (w[prv, 128:256, :].astype(F32) + ar[1].astype(F32)).astype(BF)
    reduce[5].start()

    def second_home(m, carry):
        home((m < 3) * (2 - m) + (m >= 3) * (m + 3))
        return carry

    lax.fori_loop(0, 5, second_home, 0)
    accumulate(3, False)
    gw_ref[0 : 2 * F, :] = acc[...].reshape(2 * F, QUART).astype(BF)

    def arrived(j, carry):
        rcopy(part.at[j, 0], ret.at[j], h_s.at[j], h_r.at[j], source(0)).wait_recv()
        return carry

    lax.fori_loop(0, NZ, arrived, 0)

    unit_rows = lax.broadcasted_iota(jnp.int32, (NZ * UNIT, 2 * T), 0).astype(F32)

    def last(i, carry):
        cols = pl.ds(pl.multiple_of(i * 256, 256), 256)
        rows = ret[:, :, cols].reshape(NZ * UNIT, 256)
        for half in range(2):
            pick_t = jnp.where(unit_rows == place[0:1, :] + half * SLOT, 1.0, 0.0).astype(BF)
            got = lax.dot_general(
                pick_t, rows, (((0,), (0,)), ((), ())), preferred_element_type=F32
            )
            both = got.reshape(2, T, 256).astype(BF)
            outc = pl.ds(pl.multiple_of(half * HALF + i * 256, 256), 256)
            fin_send[:, :, outc] = both
        return carry

    lax.fori_loop(0, HALF // 256, last, 0)
    final = rcopy(fin_send.at[1 - c], fin_recv, f_s, f_r, core_peer)
    final.start()
    final.wait_recv()
    gt_ref[...] = (fin_send[c].astype(F32) + fin_recv[...].astype(F32)).astype(BF)

    for j in (2, 3, 4, 5):
        reduce[j].wait_recv()
    gw_ref[2 * F :, :] = (
        w[r].astype(F32) + br[0].astype(F32) + br[1].astype(F32)
    ).astype(BF)

    for copy in exchange + reduce + [final]:
        copy.wait_send()

    def drain(k, carry):
        send_unit(k).wait_send()
        fwd_y(k).wait_send()
        fwd_d1(k).wait_send()
        fwd_d2(k).wait_send()
        send_ra(k).wait_send()
        send_rb(k).wait_send()
        y_return(k).wait_send()
        send_home(k).wait_send()
        for j in range(4):
            xq_fwd(k, j).wait_send()
        for j in (1, 2, 3):
            xt_send(k, j).wait_send()
        return carry

    lax.fori_loop(0, NZ, drain, 0)
    for g in range(4):
        for j in (1, 2, 3):
            g_send(g, j).wait_send()


def on_device(tokens, grad_out, gates, routes, w_gate, w_up, w_down):
    dma = pltpu.SemaphoreType.DMA
    vmem = pl.BlockSpec(memory_space=pltpu.VMEM)
    anyspace = pl.BlockSpec(memory_space=pl.ANY)
    flops = 2 * 1536 * D * F * 7
    grad_tokens, grads = pl.pallas_call(
        kernel,
        out_shape=(
            jax.ShapeDtypeStruct((T, D), BF),
            jax.ShapeDtypeStruct((3 * F, QUART), BF),
        ),
        in_specs=[anyspace, anyspace, vmem, vmem, anyspace, anyspace, anyspace],
        out_specs=(vmem, vmem),
        scratch_shapes=[
            pltpu.VMEM((4 * T, D), BF),
            pltpu.VMEM((2, 8, T), F32),
            pltpu.VMEM((NZ, UNIT, D), BF),
            pltpu.VMEM((NZ, 4, UNIT, D), BF),
            pltpu.VMEM((D, F), BF),
            pltpu.VMEM((D, F), BF),
            pltpu.VMEM((F, D), BF),
            pltpu.VMEM((F, 32 * UNIT), BF),
            pltpu.VMEM((NZ, 4, UNIT, HALF), BF),
            pltpu.VMEM((NZ, UNIT, HALF), BF),
            pltpu.VMEM((NZ, UNIT, HALF), BF),
            pltpu.VMEM((NZ, UNIT, HALF), BF),
            pltpu.VMEM((NZ, UNIT, HALF), BF),
            pltpu.VMEM((4, F, QUART), BF),
            pltpu.VMEM((2, 128, QUART), BF),
            pltpu.VMEM((2, F, QUART), BF),
            pltpu.VMEM((2, T, D), BF),
            pltpu.VMEM((T, D), BF),
            pltpu.VMEM((8, 2 * T), F32),
            pltpu.VMEM((NZ, UNIT, D), BF),
            pltpu.VMEM((4, 4, 2, 2, UNIT, QUART), BF),
            pltpu.VMEM((4, 4, 192, 2 * F), BF),
            pltpu.VMEM((2, F, QUART), F32),
            dma((5,)), dma((3,)), dma((3,)),
            dma((NZ,)), dma((NZ,)), dma((NZ,)), dma((NZ,)),
            dma((NZ,)), dma((NZ,)), dma((NZ,)), dma((NZ,)),
            dma((NZ,)), dma((NZ,)), dma((NZ,)), dma((NZ,)),
            dma((NZ,)), dma((NZ,)), dma((NZ,)), dma((NZ,)),
            dma((6,)), dma((6,)), dma, dma,
            dma((NZ, 4)), dma((NZ, 4)), dma((NZ, 4)), dma((NZ, 4)), dma((4, 4)), dma((4, 4)),
        ],
        compiler_params=pltpu.CompilerParams(
            collective_id=0, has_side_effects=True, vmem_limit_bytes=62 * 1024 * 1024
        ),
        cost_estimate=pl.CostEstimate(flops=flops, bytes_accessed=10_000_000, transcendentals=0),
    )(
        tokens, grad_out, gates.reshape(1, T), routes.reshape(1, T),
        w_gate[0], w_up[0], w_down[0],
    )
    return (
        grad_tokens,
        grads[:F].T[None],
        grads[F : 2 * F].T[None],
        grads[2 * F :][None],
    )


def solution(mesh):
    in_specs = (
        P(("rep", "node", "local"), None),
        P(("rep", "node", "local"), None),
        P(("rep", "node", "local"), None),
        P(("rep", "node", "local"), None),
        P(("node", "local"), None, None),
        P(("node", "local"), None, None),
        P(("node", "local"), None, None),
    )
    out_specs = (
        P(("rep", "node", "local"), None),
        P(("node", "local"), "rep", None),
        P(("node", "local"), "rep", None),
        P(("node", "local"), None, "rep"),
    )
    return jax.shard_map(
        on_device, mesh=mesh, in_specs=in_specs, out_specs=out_specs, check_vma=False
    )
```

```python
import jax
import jax.numpy as jnp
from jax import lax
from jax.experimental import pallas as pl
from jax.experimental.pallas import tpu as pltpu
from jax.sharding import PartitionSpec as P

MESH = pl.DeviceIdType.MESH
BF = jnp.bfloat16
F32 = jnp.float32

D = 3584
HALF = D // 2
QUART = D // 4
F = 256
T = 128
NZ = 8
SLOT = 24
UNIT = 2 * SLOT
NT_ROWS = (((1,), (1,)), ((), ()))


def offset_of(k):
    return ((k + 1) // 2) * (1 - 2 * ((k + 1) % 2))


def kernel(
    tok_hbm, grad_hbm, gate_ref, route_ref, wg_hbm, wu_hbm, wd_hbm,
    gt_ref, gg_ref, gu_ref, gd_ref,
    stage, meta, out, x, wg, wu, wd, at, part, rda, rdb, ry, ret, w, ar, br, fin_send, fin_recv, place,
    xt, xq, gall, acc, hz,
    loc, ex_s, ex_r, z_s, z_r, y_s, y_r, d1_s, d1_r, d2_s, d2_r,
    ra_s, ra_r, rb_s, rb_r, ryy_s, ryy_r, h_s, h_r, rs_s, rs_r, f_s, f_r,
    xs_s, xs_r, xc_s, xc_r, gs_s, gs_r,
):
    r = lax.axis_index("rep")
    z = lax.axis_index("node")
    l = lax.axis_index("local")
    y = l // 2
    c = l % 2
    pair = y // 2
    core_peer = (r, z, y * 2 + 1 - c)
    y_peer = (r, z, (y + 1 - 2 * (y % 2)) * 2 + c)
    x_next = ((r + 1) % 4, z, l)
    x_prev = ((r + 3) % 4, z, l)
    x_far = ((r + 2) % 4, z, l)
    same = 1 - (pair + c) % 2
    far = 3 - y
    dest_l = same * (y * 2 + 1 - c) + (1 - same) * (far * 2 + c)
    src_l = (1 - same) * (y * 2 + pair) + same * (far * 2 + pair)

    def dest(k):
        return (r, (z + offset_of(k) + NZ) % NZ, dest_l)

    def source(k):
        return (r, (z - offset_of(k) + NZ) % NZ, src_l)

    def rcopy(src, dst, s, q, dev):
        return pltpu.make_async_remote_copy(
            src_ref=src, dst_ref=dst, send_sem=s, recv_sem=q, device_id=dev, device_id_type=MESH
        )

    mine = pl.ds(pl.multiple_of(c * T, T), T)
    mine_g = pl.ds(pl.multiple_of(2 * T + c * T, T), T)
    local = [
        pltpu.make_async_copy(tok_hbm, stage.at[mine], loc.at[0]),
        pltpu.make_async_copy(grad_hbm, stage.at[mine_g], loc.at[1]),
        pltpu.make_async_copy(wg_hbm, wg, loc.at[2]),
        pltpu.make_async_copy(wu_hbm, wu, loc.at[3]),
        pltpu.make_async_copy(wd_hbm, wd, loc.at[4]),
    ]
    for copy in local:
        copy.start()
    row8 = lax.broadcasted_iota(jnp.int32, (8, T), 0)
    meta[c] = jnp.where(row8 == 0, route_ref[...].astype(F32), gate_ref[...])

    barrier = pltpu.get_barrier_semaphore()
    for dev in (core_peer, y_peer, x_next, x_prev, x_far):
        pl.semaphore_signal(barrier, inc=1, device_id=dev, device_id_type=MESH)

    def greet(k, carry):
        pl.semaphore_signal(barrier, inc=1, device_id=dest(k), device_id_type=MESH)
        pl.semaphore_signal(barrier, inc=1, device_id=source(k), device_id_type=MESH)
        return carry

    lax.fori_loop(0, NZ, greet, 0)
    pl.semaphore_wait(barrier, 5 + 2 * NZ)

    exchange = [
        rcopy(meta.at[c], meta.at[c], ex_s.at[0], ex_r.at[0], core_peer),
        rcopy(tok_hbm, stage.at[mine], ex_s.at[1], ex_r.at[1], core_peer),
        rcopy(grad_hbm, stage.at[mine_g], ex_s.at[2], ex_r.at[2], core_peer),
    ]
    for copy in exchange:
        copy.start()
    exchange[0].wait_recv()
    route = jnp.concatenate([meta[0, 0:1, :], meta[1, 0:1, :]], axis=1)
    gate = jnp.concatenate([meta[0, 1:2, :], meta[1, 1:2, :]], axis=1)
    expert = lax.broadcasted_iota(jnp.int32, (16, 2 * T), 0)
    wanted = jnp.where(expert < NZ, 2 * expert + c, -1).astype(F32)
    match = jnp.where(route == wanted, 1.0, 0.0)
    earlier = lax.broadcasted_iota(jnp.int32, (2 * T, 2 * T), 0) < lax.broadcasted_iota(
        jnp.int32, (2 * T, 2 * T), 1
    )
    before = jnp.dot(
        match.astype(BF), jnp.where(earlier, 1.0, 0.0).astype(BF), preferred_element_type=F32
    )
    position = jnp.sum(before * match, axis=0, keepdims=True)
    number = jnp.sum(expert.astype(F32) * match, axis=0, keepdims=True)
    known = jnp.sum(match, axis=0, keepdims=True) > 0.5
    target = jnp.where(known, number * SLOT + position, -1.0)
    slots = lax.broadcasted_iota(jnp.int32, (NZ * SLOT, 2 * T), 0).astype(F32)
    chosen = slots == target
    slot_gate = jnp.sum(jnp.where(chosen, gate, 0.0), axis=1, keepdims=True)
    pick = jnp.where(chosen, 1.0, 0.0).astype(BF)
    local[0].wait()
    local[1].wait()
    exchange[1].wait_recv()
    exchange[2].wait_recv()

    def pack(i, carry):
        cols = pl.ds(pl.multiple_of(i * 512, 512), 512)
        rows = jnp.dot(pick, stage[0 : 2 * T, cols], preferred_element_type=F32)
        ups = jnp.dot(pick, stage[2 * T : 4 * T, cols], preferred_element_type=F32) * slot_gate
        both = jnp.concatenate(
            [rows.reshape(NZ, SLOT, 512), ups.reshape(NZ, SLOT, 512)], axis=1
        )
        out[:, :, cols] = both.astype(BF)
        return carry

    lax.fori_loop(0, D // 512, pack, 0)

    def half_cols(h):
        return pl.ds(pl.multiple_of(h * HALF, 128), HALF)

    def send_unit(k, h):
        return rcopy(
            out.at[(z + offset_of(k) + NZ) % NZ, :, half_cols(h)], x.at[k, 0, :, half_cols(h)],
            z_s.at[k, h], z_r.at[k, h], dest(k),
        )

    def fwd_y(k, h):
        return rcopy(
            x.at[k, 0, :, half_cols(h)], x.at[k, 1, :, half_cols(h)],
            y_s.at[k, h], y_r.at[k, h], y_peer,
        )

    def fwd_d1(k):
        return rcopy(x.at[k, 0], x.at[k, 2], d1_s.at[k], d1_r.at[k], core_peer)

    def fwd_d2(k):
        return rcopy(x.at[k, 1], x.at[k, 3], d2_s.at[k], d2_r.at[k], core_peer)

    def send_one(k, carry):
        send_unit(k, 0).start()
        send_unit(k, 1).start()
        return carry

    lax.fori_loop(0, NZ, send_one, 0)
    for copy in local[2:]:
        copy.wait()
    back = jnp.where(known, number * UNIT + position, -1000.0)
    unit_rows = lax.broadcasted_iota(jnp.int32, (NZ * UNIT, 2 * T), 0).astype(F32)
    for half in range(2):
        place[half] = jnp.where(unit_rows == back + half * SLOT, 1.0, 0.0).T.astype(BF)

    def forward_unit(k):
        rows = x[k].reshape(4 * UNIT, D)
        pre_g = jnp.dot(rows, wg[...], preferred_element_type=F32)
        pre_u = jnp.dot(rows, wu[...], preferred_element_type=F32)
        gh = lax.dot_general(rows, wd[...], NT_ROWS, preferred_element_type=F32)
        a = pre_g.reshape(4, UNIT, F)[:, :SLOT]
        u = pre_u.reshape(4, UNIT, F)[:, :SLOT]
        h = gh.reshape(4, UNIT, F)[:, SLOT:]
        sigma = 1.0 / (1.0 + jnp.exp(-a))
        swish = a * sigma
        hidden = swish * u
        d_gate = h * u * sigma * (1.0 + a * (1.0 - sigma))
        d_up = h * swish
        gall[k // 2, 0, k % 2, :, 0:F] = d_gate.reshape(96, F).astype(BF)
        gall[k // 2, 0, k % 2, :, F : 2 * F] = d_up.reshape(96, F).astype(BF)
        both = jnp.concatenate([jnp.zeros_like(hidden), hidden], axis=1)
        hz[k] = both.reshape(4 * UNIT, F).astype(BF)

    def quarter(q):
        return pl.ds(pl.multiple_of(q * QUART, 128), QUART)

    def xt_send(k, j):
        return rcopy(
            xt.at[k, :, quarter((r + j) % 4)], xq.at[k // 2, 4 - j, k % 2, 0],
            xs_s.at[k, j], xs_r.at[k, 4 - j], ((r + j) % 4, z, l),
        )

    def xt_got(k, j):
        return rcopy(
            xt.at[k, :, quarter(r)], xq.at[k // 2, j, k % 2, 0],
            xs_s.at[k, j], xs_r.at[k, j], ((r + j) % 4, z, l),
        )

    def xq_fwd(k, j):
        src = xt.at[k, :, quarter(r)] if j == 0 else xq.at[k // 2, j, k % 2, 0]
        return rcopy(src, xq.at[k // 2, j, k % 2, 1], xc_s.at[k, j], xc_r.at[k, j], core_peer)

    def g_send(k, j):
        return rcopy(
            gall.at[k // 2, 0, k % 2], gall.at[k // 2, 4 - j, k % 2],
            gs_s.at[k, j], gs_r.at[k, 4 - j], ((r + j) % 4, z, l),
        )

    def g_got(k, j):
        return rcopy(
            gall.at[k // 2, 0, k % 2], gall.at[k // 2, j, k % 2],
            gs_s.at[k, j], gs_r.at[k, j], ((r + j) % 4, z, l),
        )

    def compact(k):
        def columns(i, carry):
            cols = pl.ds(pl.multiple_of(i * QUART, 128), QUART)
            both = x[k, 0:2, :, cols].astype(F32)[:, :SLOT]
            xt[k, :, cols] = both.reshape(UNIT, QUART).astype(BF)
            return carry

        lax.fori_loop(0, 4, columns, 0)
        xq[k // 2, 0, k % 2, 0] = xt[k, :, quarter(r)]
        for j in (2, 1, 3):
            xt_send(k, j).start()
        xq_fwd(k, 0).start()

    def relay_quarters(k):
        for j in (1, 2, 3):
            xt_got(k, j).wait_recv()
            xq_fwd(k, j).start()

    def accumulate(g, first):
        for kk in range(2):
            for j in range(4):
                xq_fwd(2 * g + kk, j).wait_recv()
            for j in (1, 2, 3):
                g_got(2 * g + kk, j).wait_recv()
        rows = xq[g].reshape(4 * 192, QUART)
        for m in range(2):
            left = gall[g, :, :, :, m * F : (m + 1) * F].reshape(4 * 192, F)
            term = lax.dot_general(left, rows, (((0,), (0,)), ((), ())), preferred_element_type=F32)
            if first:
                acc[m] = term
            else:
                acc[m] += term

    def send_ra(k):
        return rcopy(part.at[k, 2], rda.at[k], ra_s.at[k], ra_r.at[k], core_peer)

    def send_rb(k):
        return rcopy(part.at[k, 3], rdb.at[k], rb_s.at[k], rb_r.at[k], core_peer)

    def route_unit(k):
        left = gall[k // 2, 0, k % 2, :, 0:F]
        right = gall[k // 2, 0, k % 2, :, F : 2 * F]

        def columns(i, carry):
            done = []
            for half in range(2):
                cols = pl.ds(pl.multiple_of(half * HALF + i * 256, 256), 256)
                one = lax.dot_general(left, wg[cols, :], NT_ROWS, preferred_element_type=F32)
                one += lax.dot_general(right, wu[cols, :], NT_ROWS, preferred_element_type=F32)
                done.append(one.reshape(4, SLOT, 256))
            part[k, :, :, pl.ds(pl.multiple_of(i * 256, 256), 256)] = (
                jnp.concatenate(done, axis=1).astype(BF)
            )
            return carry

        lax.fori_loop(0, HALF // 256, columns, 0)
        send_rb(k).start()
        send_ra(k).start()

    def y_return(k):
        return rcopy(part.at[k, 1], ry.at[k], ryy_s.at[k], ryy_r.at[k], y_peer)

    def across(k):
        send_rb(k).wait_recv()
        part[k, 1] = (part[k, 1].astype(F32) + rdb[k].astype(F32)).astype(BF)
        y_return(k).start()

    def send_home(k):
        return rcopy(part.at[k, 0], ret.at[z], h_s.at[k], h_r.at[z], source(k))

    def home(k):
        send_ra(k).wait_recv()
        y_return(k).wait_recv()
        part[k, 0] = (
            part[k, 0].astype(F32) + rda[k].astype(F32) + ry[k].astype(F32)
        ).astype(BF)
        send_home(k).start()

    def relay(k):
        for h in range(2):
            send_unit(k, h).wait_recv()
            fwd_y(k, h).start()
        fwd_d1(k).start()

    def turn(t, carry):
        k = t - 1

        @pl.when(t < NZ - 1)
        def _():
            relay(t)

        @pl.when(t > 0)
        def _():
            fwd_y(k, 0).wait_recv()
            fwd_y(k, 1).wait_recv()
            fwd_d2(k).start()
            compact(k)
            fwd_d1(k).wait_recv()
            fwd_d2(k).wait_recv()
            forward_unit(k)
            route_unit(k)
            for j in (2, 1, 3):
                g_send(k, j).start()

        @pl.when((t > 0) & (t < NZ))
        def _():
            across(k)

        @pl.when(t > 2)
        def _():
            relay_quarters(t - 3)

        @pl.when(t == 5)
        def _():
            accumulate(0, True)

        @pl.when(t == 7)
        def _():
            accumulate(1, False)
            relay(7)

            def early(m, carry):
                home(5 - m)
                return carry

            lax.fori_loop(0, 6, early, 0)

        return carry

    lax.fori_loop(0, NZ + 1, turn, 0)
    at[...] = hz[...].reshape(32 * UNIT, F).T

    def weight_chunk(q):
        rows = x[:, :, :, quarter(q)].reshape(32 * UNIT, QUART)
        w[q] = jnp.dot(at[...], rows, preferred_element_type=F32).astype(BF)

    opposite, nxt, prv = (r + 2) % 4, (r + 1) % 4, (r + 3) % 4
    low, high = pl.ds(0, 128), pl.ds(128, 128)
    reduce = [
        rcopy(w.at[opposite, low], ar.at[0], rs_s.at[0], rs_r.at[0], x_next),
        rcopy(w.at[opposite, high], ar.at[1], rs_s.at[1], rs_r.at[1], x_prev),
        rcopy(w.at[nxt, high], br.at[0, high], rs_s.at[2], rs_r.at[2], x_next),
        rcopy(w.at[prv, low], br.at[1, low], rs_s.at[3], rs_r.at[3], x_prev),
        rcopy(w.at[nxt, low], br.at[0, low], rs_s.at[4], rs_r.at[4], x_next),
        rcopy(w.at[prv, high], br.at[1, high], rs_s.at[5], rs_r.at[5], x_prev),
    ]

    def step(j, carry):
        weight_chunk((r + (2 + j) * (j < 2) + (3 - j) * (j >= 2)) % 4)

        @pl.when(j == 0)
        def _():
            reduce[0].start()
            reduce[1].start()
            across(7)
            home(6)

        @pl.when(j == 1)
        def _():
            reduce[3].start()

        @pl.when(j == 2)
        def _():
            reduce[2].start()

        return carry

    lax.fori_loop(0, 4, step, 0)
    accumulate(2, False)
    home(7)
    relay_quarters(6)
    relay_quarters(7)

    reduce[0].wait_recv()
    w[nxt, 0:128, :] = (w[nxt, 0:128, :].astype(F32) + ar[0].astype(F32)).astype(BF)
    reduce[4].start()
    reduce[1].wait_recv()
    w[prv, 128:256, :] = (w[prv, 128:256, :].astype(F32) + ar[1].astype(F32)).astype(BF)
    reduce[5].start()
    accumulate(3, False)
    gg_ref[...] = acc[0].T.astype(BF)
    gu_ref[...] = acc[1].T.astype(BF)

    def arrived(j, carry):
        rcopy(part.at[j, 0], ret.at[j], h_s.at[j], h_r.at[j], source(0)).wait_recv()
        return carry

    lax.fori_loop(0, NZ, arrived, 0)

    def final(half):
        cols = pl.ds(half * HALF, HALF)
        return rcopy(
            fin_send.at[1 - c, :, cols], fin_recv.at[:, cols], f_s.at[half], f_r.at[half], core_peer
        )

    for half in range(2):

        def last(i, carry):
            cols = pl.ds(pl.multiple_of(i * 256, 256), 256)
            rows = ret[:, :, cols].reshape(NZ * UNIT, 256)
            got = jnp.dot(place[half], rows, preferred_element_type=F32)
            outc = pl.ds(pl.multiple_of(half * HALF + i * 256, 256), 256)
            fin_send[:, :, outc] = got.reshape(2, T, 256).astype(BF)
            return carry

        lax.fori_loop(0, HALF // 256, last, 0)
        final(half).start()

    for j in (2, 3, 4, 5):
        reduce[j].wait_recv()
    gd_ref[...] = (
        w[r].astype(F32) + br[0].astype(F32) + br[1].astype(F32)
    ).astype(BF)

    for half in range(2):
        final(half).wait_recv()
        cols = slice(half * HALF, (half + 1) * HALF)
        gt_ref[:, cols] = (
            fin_send[c, :, cols].astype(F32) + fin_recv[:, cols].astype(F32)
        ).astype(BF)

    for copy in exchange + reduce + [final(0), final(1)]:
        copy.wait_send()

    def drain(k, carry):
        for h in range(2):
            send_unit(k, h).wait_send()
            fwd_y(k, h).wait_send()
        fwd_d1(k).wait_send()
        fwd_d2(k).wait_send()
        send_ra(k).wait_send()
        send_rb(k).wait_send()
        y_return(k).wait_send()
        send_home(k).wait_send()
        for j in range(4):
            xq_fwd(k, j).wait_send()
        for j in (1, 2, 3):
            xt_send(k, j).wait_send()
            g_send(k, j).wait_send()
        return carry

    lax.fori_loop(0, NZ, drain, 0)


def on_device(tokens, grad_out, gates, routes, w_gate, w_up, w_down):
    dma = pltpu.SemaphoreType.DMA
    vmem = pl.BlockSpec(memory_space=pltpu.VMEM)
    anyspace = pl.BlockSpec(memory_space=pl.ANY)
    flops = 2 * 1536 * D * F * 7
    grad_tokens, grad_gate, grad_up, grad_down = pl.pallas_call(
        kernel,
        out_shape=(
            jax.ShapeDtypeStruct((T, D), BF),
            jax.ShapeDtypeStruct((QUART, F), BF),
            jax.ShapeDtypeStruct((QUART, F), BF),
            jax.ShapeDtypeStruct((F, QUART), BF),
        ),
        in_specs=[anyspace, anyspace, vmem, vmem, anyspace, anyspace, anyspace],
        out_specs=(vmem, vmem, vmem, vmem),
        scratch_shapes=[
            pltpu.VMEM((4 * T, D), BF),
            pltpu.VMEM((2, 8, T), F32),
            pltpu.VMEM((NZ, UNIT, D), BF),
            pltpu.VMEM((NZ, 4, UNIT, D), BF),
            pltpu.VMEM((D, F), BF),
            pltpu.VMEM((D, F), BF),
            pltpu.VMEM((F, D), BF),
            pltpu.VMEM((F, 32 * UNIT), BF),
            pltpu.VMEM((NZ, 4, UNIT, HALF), BF),
            pltpu.VMEM((NZ, UNIT, HALF), BF),
            pltpu.VMEM((NZ, UNIT, HALF), BF),
            pltpu.VMEM((NZ, UNIT, HALF), BF),
            pltpu.VMEM((NZ, UNIT, HALF), BF),
            pltpu.VMEM((4, F, QUART), BF),
            pltpu.VMEM((2, 128, QUART), BF),
            pltpu.VMEM((2, F, QUART), BF),
            pltpu.VMEM((2, T, D), BF),
            pltpu.VMEM((T, D), BF),
            pltpu.VMEM((2, 2 * T, NZ * UNIT), BF),
            pltpu.VMEM((NZ, UNIT, D), BF),
            pltpu.VMEM((4, 4, 2, 2, UNIT, QUART), BF),
            pltpu.VMEM((4, 4, 2, 96, 2 * F), BF),
            pltpu.VMEM((2, F, QUART), F32),
            pltpu.VMEM((NZ, 4 * UNIT, F), BF),
            dma((5,)), dma((3,)), dma((3,)),
            dma((NZ, 2)), dma((NZ, 2)), dma((NZ, 2)), dma((NZ, 2)),
            dma((NZ,)), dma((NZ,)), dma((NZ,)), dma((NZ,)),
            dma((NZ,)), dma((NZ,)), dma((NZ,)), dma((NZ,)),
            dma((NZ,)), dma((NZ,)), dma((NZ,)), dma((NZ,)),
            dma((6,)), dma((6,)), dma((2,)), dma((2,)),
            dma((NZ, 4)), dma((NZ, 4)), dma((NZ, 4)), dma((NZ, 4)), dma((NZ, 4)), dma((NZ, 4)),
        ],
        compiler_params=pltpu.CompilerParams(
            collective_id=0, has_side_effects=True, vmem_limit_bytes=62 * 1024 * 1024
        ),
        cost_estimate=pl.CostEstimate(flops=flops, bytes_accessed=10_000_000, transcendentals=0),
    )(
        tokens, grad_out, gates.reshape(1, T), routes.reshape(1, T),
        w_gate[0], w_up[0], w_down[0],
    )
    return (grad_tokens, grad_gate[None], grad_up[None], grad_down[None])


def solution(mesh):
    in_specs = (
        P(("rep", "node", "local"), None),
        P(("rep", "node", "local"), None),
        P(("rep", "node", "local"), None),
        P(("rep", "node", "local"), None),
        P(("node", "local"), None, None),
        P(("node", "local"), None, None),
        P(("node", "local"), None, None),
    )
    out_specs = (
        P(("rep", "node", "local"), None),
        P(("node", "local"), "rep", None),
        P(("node", "local"), "rep", None),
        P(("node", "local"), None, "rep"),
    )
    return jax.shard_map(
        on_device, mesh=mesh, in_specs=in_specs, out_specs=out_specs, check_vma=False
    )
```

```python
import jax
import jax.numpy as jnp
from jax import lax
from jax.experimental import pallas as pl
from jax.experimental.pallas import tpu as pltpu
from jax.sharding import PartitionSpec as P

MESH = pl.DeviceIdType.MESH
BF = jnp.bfloat16
F32 = jnp.float32

D = 3584
HALF = D // 2
QUART = D // 4
F = 256
T = 128
NZ = 8
SLOT = 24
UNIT = 2 * SLOT
NT_ROWS = (((1,), (1,)), ((), ()))


def offset_of(k):
    return ((k + 1) // 2) * (1 - 2 * ((k + 1) % 2))


def kernel(
    tok_hbm, grad_hbm, gate_ref, route_ref, wg_hbm, wu_hbm, wd_hbm,
    gt_ref, gg_ref, gu_ref, gd_ref,
    stage, meta, out, x, wg, wu, wd, at, part, rda, rdb, ry, ret, w, ar, br, fin_send, fin_recv, place,
    xt, xq, gall, acc, hz,
    loc, ex_s, ex_r, z_s, z_r, y_s, y_r, d1_s, d1_r, d2_s, d2_r,
    ra_s, ra_r, rb_s, rb_r, ryy_s, ryy_r, h_s, h_r, rs_s, rs_r, f_s, f_r,
    xs_s, xs_r, xc_s, xc_r, gs_s, gs_r,
):
    r = lax.axis_index("rep")
    z = lax.axis_index("node")
    l = lax.axis_index("local")
    y = l // 2
    c = l % 2
    pair = y // 2
    core_peer = (r, z, y * 2 + 1 - c)
    y_peer = (r, z, (y + 1 - 2 * (y % 2)) * 2 + c)
    x_next = ((r + 1) % 4, z, l)
    x_prev = ((r + 3) % 4, z, l)
    x_far = ((r + 2) % 4, z, l)
    same = 1 - (pair + c) % 2
    far = 3 - y
    dest_l = same * (y * 2 + 1 - c) + (1 - same) * (far * 2 + c)
    src_l = (1 - same) * (y * 2 + pair) + same * (far * 2 + pair)

    def dest(k):
        return (r, (z + offset_of(k) + NZ) % NZ, dest_l)

    def source(k):
        return (r, (z - offset_of(k) + NZ) % NZ, src_l)

    def rcopy(src, dst, s, q, dev):
        return pltpu.make_async_remote_copy(
            src_ref=src, dst_ref=dst, send_sem=s, recv_sem=q, device_id=dev, device_id_type=MESH
        )

    mine = pl.ds(pl.multiple_of(c * T, T), T)
    mine_g = pl.ds(pl.multiple_of(2 * T + c * T, T), T)
    local = [
        pltpu.make_async_copy(tok_hbm, stage.at[mine], loc.at[0]),
        pltpu.make_async_copy(grad_hbm, stage.at[mine_g], loc.at[1]),
        pltpu.make_async_copy(wg_hbm, wg, loc.at[2]),
        pltpu.make_async_copy(wu_hbm, wu, loc.at[3]),
        pltpu.make_async_copy(wd_hbm, wd, loc.at[4]),
    ]
    for copy in local:
        copy.start()
    row8 = lax.broadcasted_iota(jnp.int32, (8, T), 0)
    meta[c] = jnp.where(row8 == 0, route_ref[...].astype(F32), gate_ref[...])

    barrier = pltpu.get_barrier_semaphore()
    for dev in (core_peer, y_peer, x_next, x_prev, x_far):
        pl.semaphore_signal(barrier, inc=1, device_id=dev, device_id_type=MESH)

    def greet(k, carry):
        pl.semaphore_signal(barrier, inc=1, device_id=dest(k), device_id_type=MESH)
        pl.semaphore_signal(barrier, inc=1, device_id=source(k), device_id_type=MESH)
        return carry

    lax.fori_loop(0, NZ, greet, 0)
    pl.semaphore_wait(barrier, 5 + 2 * NZ)

    exchange = [
        rcopy(meta.at[c], meta.at[c], ex_s.at[0], ex_r.at[0], core_peer),
        rcopy(tok_hbm, stage.at[mine], ex_s.at[1], ex_r.at[1], core_peer),
        rcopy(grad_hbm, stage.at[mine_g], ex_s.at[2], ex_r.at[2], core_peer),
    ]
    for copy in exchange:
        copy.start()
    exchange[0].wait_recv()
    route = jnp.concatenate([meta[0, 0:1, :], meta[1, 0:1, :]], axis=1)
    gate = jnp.concatenate([meta[0, 1:2, :], meta[1, 1:2, :]], axis=1)
    expert = lax.broadcasted_iota(jnp.int32, (16, 2 * T), 0)
    wanted = jnp.where(expert < NZ, 2 * expert + c, -1).astype(F32)
    match = jnp.where(route == wanted, 1.0, 0.0)
    earlier = lax.broadcasted_iota(jnp.int32, (2 * T, 2 * T), 0) < lax.broadcasted_iota(
        jnp.int32, (2 * T, 2 * T), 1
    )
    before = jnp.dot(
        match.astype(BF), jnp.where(earlier, 1.0, 0.0).astype(BF), preferred_element_type=F32
    )
    position = jnp.sum(before * match, axis=0, keepdims=True)
    number = jnp.sum(expert.astype(F32) * match, axis=0, keepdims=True)
    known = jnp.sum(match, axis=0, keepdims=True) > 0.5
    target = jnp.where(known, number * SLOT + position, -1.0)
    slots = lax.broadcasted_iota(jnp.int32, (NZ * SLOT, 2 * T), 0).astype(F32)
    chosen = slots == target
    slot_gate = jnp.sum(jnp.where(chosen, gate, 0.0), axis=1, keepdims=True)
    pick = jnp.where(chosen, 1.0, 0.0).astype(BF)
    local[0].wait()
    local[1].wait()
    exchange[1].wait_recv()
    exchange[2].wait_recv()

    def pack(i, carry):
        cols = pl.ds(pl.multiple_of(i * 512, 512), 512)
        rows = jnp.dot(pick, stage[0 : 2 * T, cols], preferred_element_type=F32)
        ups = jnp.dot(pick, stage[2 * T : 4 * T, cols], preferred_element_type=F32) * slot_gate
        both = jnp.concatenate(
            [rows.reshape(NZ, SLOT, 512), ups.reshape(NZ, SLOT, 512)], axis=1
        )
        out[:, :, cols] = both.astype(BF)
        return carry

    lax.fori_loop(0, D // 512, pack, 0)

    def half_cols(h):
        return pl.ds(pl.multiple_of(h * HALF, 128), HALF)

    def send_unit(k, h):
        return rcopy(
            out.at[(z + offset_of(k) + NZ) % NZ, :, half_cols(h)], x.at[k, 0, :, half_cols(h)],
            z_s.at[k, h], z_r.at[k, h], dest(k),
        )

    def fwd_y(k, h):
        return rcopy(
            x.at[k, 0, :, half_cols(h)], x.at[k, 1, :, half_cols(h)],
            y_s.at[k, h], y_r.at[k, h], y_peer,
        )

    def fwd_d1(k):
        return rcopy(x.at[k, 0], x.at[k, 2], d1_s.at[k], d1_r.at[k], core_peer)

    def fwd_d2(k):
        return rcopy(x.at[k, 1], x.at[k, 3], d2_s.at[k], d2_r.at[k], core_peer)

    def send_one(k, carry):
        send_unit(k, 0).start()
        send_unit(k, 1).start()
        return carry

    lax.fori_loop(0, NZ, send_one, 0)
    for copy in local[2:]:
        copy.wait()
    back = jnp.where(known, number * UNIT + position, -1000.0)
    unit_rows = lax.broadcasted_iota(jnp.int32, (NZ * UNIT, 2 * T), 0).astype(F32)
    for half in range(2):
        place[half] = jnp.where(unit_rows == back + half * SLOT, 1.0, 0.0).T.astype(BF)

    def forward_units(k, n):
        these = pl.ds(k, n)
        rows = x[these].reshape(n * 4 * UNIT, D)
        pre_g = jnp.dot(rows, wg[...], preferred_element_type=F32)
        pre_u = jnp.dot(rows, wu[...], preferred_element_type=F32)
        gh = lax.dot_general(rows, wd[...], NT_ROWS, preferred_element_type=F32)
        a = pre_g.reshape(n * 4, UNIT, F)[:, :SLOT]
        u = pre_u.reshape(n * 4, UNIT, F)[:, :SLOT]
        h = gh.reshape(n * 4, UNIT, F)[:, SLOT:]
        sigma = 1.0 / (1.0 + jnp.exp(-a))
        swish = a * sigma
        hidden = swish * u
        d_gate = h * u * sigma * (1.0 + a * (1.0 - sigma))
        d_up = h * swish
        place_g = pl.ds(k % 2, n)
        gall[k // 2, 0, place_g, :, 0:F] = d_gate.reshape(n, 96, F).astype(BF)
        gall[k // 2, 0, place_g, :, F : 2 * F] = d_up.reshape(n, 96, F).astype(BF)
        both = jnp.concatenate([jnp.zeros_like(hidden), hidden], axis=1)
        hz[these] = both.reshape(n, 4 * UNIT, F).astype(BF)

    def quarter(q):
        return pl.ds(pl.multiple_of(q * QUART, 128), QUART)

    def xt_send(k, j):
        return rcopy(
            xt.at[k, :, quarter((r + j) % 4)], xq.at[k // 2, 4 - j, k % 2, 0],
            xs_s.at[k, j], xs_r.at[k, 4 - j], ((r + j) % 4, z, l),
        )

    def xt_got(k, j):
        return rcopy(
            xt.at[k, :, quarter(r)], xq.at[k // 2, j, k % 2, 0],
            xs_s.at[k, j], xs_r.at[k, j], ((r + j) % 4, z, l),
        )

    def xq_fwd(k, j):
        src = xt.at[k, :, quarter(r)] if j == 0 else xq.at[k // 2, j, k % 2, 0]
        return rcopy(src, xq.at[k // 2, j, k % 2, 1], xc_s.at[k, j], xc_r.at[k, j], core_peer)

    def g_send(k, j):
        return rcopy(
            gall.at[k // 2, 0, k % 2], gall.at[k // 2, 4 - j, k % 2],
            gs_s.at[k, j], gs_r.at[k, 4 - j], ((r + j) % 4, z, l),
        )

    def g_got(k, j):
        return rcopy(
            gall.at[k // 2, 0, k % 2], gall.at[k // 2, j, k % 2],
            gs_s.at[k, j], gs_r.at[k, j], ((r + j) % 4, z, l),
        )

    def compact(k):
        def columns(i, carry):
            cols = pl.ds(pl.multiple_of(i * QUART, 128), QUART)
            both = x[k, 0:2, :, cols].astype(F32)[:, :SLOT]
            xt[k, :, cols] = both.reshape(UNIT, QUART).astype(BF)
            return carry

        lax.fori_loop(0, 4, columns, 0)
        xq[k // 2, 0, k % 2, 0] = xt[k, :, quarter(r)]
        for j in (2, 1, 3):
            xt_send(k, j).start()
        xq_fwd(k, 0).start()

    def relay_quarters(k):
        for j in (1, 2, 3):
            xt_got(k, j).wait_recv()
            xq_fwd(k, j).start()

    def accumulate(g, first):
        for kk in range(2):
            for j in range(4):
                xq_fwd(2 * g + kk, j).wait_recv()
            for j in (1, 2, 3):
                g_got(2 * g + kk, j).wait_recv()
        rows = xq[g].reshape(4 * 192, QUART)
        for m in range(2):
            left = gall[g, :, :, :, m * F : (m + 1) * F].reshape(4 * 192, F)
            term = lax.dot_general(left, rows, (((0,), (0,)), ((), ())), preferred_element_type=F32)
            if first:
                acc[m] = term
            else:
                acc[m] += term

    def send_ra(k):
        return rcopy(part.at[k, 2], rda.at[k], ra_s.at[k], ra_r.at[k], core_peer)

    def send_rb(k):
        return rcopy(part.at[k, 3], rdb.at[k], rb_s.at[k], rb_r.at[k], core_peer)

    def route_units(k, n):
        left = gall[k // 2, 0, pl.ds(k % 2, n), :, 0:F].reshape(n * 96, F)
        right = gall[k // 2, 0, pl.ds(k % 2, n), :, F : 2 * F].reshape(n * 96, F)

        def columns(i, carry):
            done = []
            for half in range(2):
                cols = pl.ds(pl.multiple_of(half * HALF + i * 256, 256), 256)
                one = lax.dot_general(left, wg[cols, :], NT_ROWS, preferred_element_type=F32)
                one += lax.dot_general(right, wu[cols, :], NT_ROWS, preferred_element_type=F32)
                done.append(one.reshape(n, 4, SLOT, 256))
            part[pl.ds(k, n), :, :, pl.ds(pl.multiple_of(i * 256, 256), 256)] = (
                jnp.concatenate(done, axis=2).astype(BF)
            )
            return carry

        lax.fori_loop(0, HALF // 256, columns, 0)
        for i in range(n):
            send_rb(k + i).start()
            send_ra(k + i).start()
            for j in (2, 1, 3):
                g_send(k + i, j).start()

    def y_return(k):
        return rcopy(part.at[k, 1], ry.at[k], ryy_s.at[k], ryy_r.at[k], y_peer)

    def across(k):
        send_rb(k).wait_recv()
        part[k, 1] = (part[k, 1].astype(F32) + rdb[k].astype(F32)).astype(BF)
        y_return(k).start()

    def send_home(k):
        return rcopy(part.at[k, 0], ret.at[z], h_s.at[k], h_r.at[z], source(k))

    def home(k):
        send_ra(k).wait_recv()
        y_return(k).wait_recv()
        part[k, 0] = (
            part[k, 0].astype(F32) + rda[k].astype(F32) + ry[k].astype(F32)
        ).astype(BF)
        send_home(k).start()

    def relay(k):
        for h in range(2):
            send_unit(k, h).wait_recv()
            fwd_y(k, h).start()
        fwd_d1(k).start()

    def turn(t, carry):
        k = t - 1

        @pl.when(t < NZ - 1)
        def _():
            relay(t)

        @pl.when(t > 0)
        def _():
            fwd_y(k, 0).wait_recv()
            fwd_y(k, 1).wait_recv()
            fwd_d2(k).start()
            compact(k)

        @pl.when((t > 0) & (t < NZ - 1) & (t % 2 == 0))
        def _():
            for i in range(2):
                fwd_d1(t - 2 + i).wait_recv()
                fwd_d2(t - 2 + i).wait_recv()
            forward_units(t - 2, 2)
            route_units(t - 2, 2)
            across(t - 2)
            across(t - 1)

        @pl.when(t >= NZ - 1)
        def _():
            fwd_d1(k).wait_recv()
            fwd_d2(k).wait_recv()
            forward_units(k, 1)
            route_units(k, 1)

        @pl.when(t == NZ - 1)
        def _():
            across(NZ - 2)

        @pl.when(t > 2)
        def _():
            relay_quarters(t - 3)

        @pl.when(t == 5)
        def _():
            accumulate(0, True)

        @pl.when(t == 7)
        def _():
            accumulate(1, False)
            relay(7)

            def early(m, carry):
                home(5 - m)
                return carry

            lax.fori_loop(0, 6, early, 0)

        return carry

    lax.fori_loop(0, NZ + 1, turn, 0)
    at[...] = hz[...].reshape(32 * UNIT, F).T

    def weight_chunk(q):
        rows = x[:, :, :, quarter(q)].reshape(32 * UNIT, QUART)
        w[q] = jnp.dot(at[...], rows, preferred_element_type=F32).astype(BF)

    opposite, nxt, prv = (r + 2) % 4, (r + 1) % 4, (r + 3) % 4
    low, high = pl.ds(0, 128), pl.ds(128, 128)
    reduce = [
        rcopy(w.at[opposite, low], ar.at[0], rs_s.at[0], rs_r.at[0], x_next),
        rcopy(w.at[opposite, high], ar.at[1], rs_s.at[1], rs_r.at[1], x_prev),
        rcopy(w.at[nxt, high], br.at[0, high], rs_s.at[2], rs_r.at[2], x_next),
        rcopy(w.at[prv, low], br.at[1, low], rs_s.at[3], rs_r.at[3], x_prev),
        rcopy(w.at[nxt, low], br.at[0, low], rs_s.at[4], rs_r.at[4], x_next),
        rcopy(w.at[prv, high], br.at[1, high], rs_s.at[5], rs_r.at[5], x_prev),
    ]

    def step(j, carry):
        weight_chunk((r + (2 + j) * (j < 2) + (3 - j) * (j >= 2)) % 4)

        @pl.when(j == 0)
        def _():
            reduce[0].start()
            reduce[1].start()
            across(7)
            home(6)

        @pl.when(j == 1)
        def _():
            reduce[3].start()

        @pl.when(j == 2)
        def _():
            reduce[2].start()

        return carry

    lax.fori_loop(0, 4, step, 0)
    accumulate(2, False)
    home(7)
    relay_quarters(6)
    relay_quarters(7)

    reduce[0].wait_recv()
    w[nxt, 0:128, :] = (w[nxt, 0:128, :].astype(F32) + ar[0].astype(F32)).astype(BF)
    reduce[4].start()
    reduce[1].wait_recv()
    w[prv, 128:256, :] = (w[prv, 128:256, :].astype(F32) + ar[1].astype(F32)).astype(BF)
    reduce[5].start()
    accumulate(3, False)
    gg_ref[...] = acc[0].T.astype(BF)
    gu_ref[...] = acc[1].T.astype(BF)

    def arrived(j, carry):
        rcopy(part.at[j, 0], ret.at[j], h_s.at[j], h_r.at[j], source(0)).wait_recv()
        return carry

    lax.fori_loop(0, NZ, arrived, 0)

    def final(half):
        cols = pl.ds(half * HALF, HALF)
        return rcopy(
            fin_send.at[1 - c, :, cols], fin_recv.at[:, cols], f_s.at[half], f_r.at[half], core_peer
        )

    for half in range(2):

        def last(i, carry):
            cols = pl.ds(pl.multiple_of(i * 256, 256), 256)
            rows = ret[:, :, cols].reshape(NZ * UNIT, 256)
            got = jnp.dot(place[half], rows, preferred_element_type=F32)
            outc = pl.ds(pl.multiple_of(half * HALF + i * 256, 256), 256)
            fin_send[:, :, outc] = got.reshape(2, T, 256).astype(BF)
            return carry

        lax.fori_loop(0, HALF // 256, last, 0)
        final(half).start()

    for j in (2, 3, 4, 5):
        reduce[j].wait_recv()
    gd_ref[...] = (
        w[r].astype(F32) + br[0].astype(F32) + br[1].astype(F32)
    ).astype(BF)

    for half in range(2):
        final(half).wait_recv()
        cols = slice(half * HALF, (half + 1) * HALF)
        gt_ref[:, cols] = (
            fin_send[c, :, cols].astype(F32) + fin_recv[:, cols].astype(F32)
        ).astype(BF)

    for copy in exchange + reduce + [final(0), final(1)]:
        copy.wait_send()

    def drain(k, carry):
        for h in range(2):
            send_unit(k, h).wait_send()
            fwd_y(k, h).wait_send()
        fwd_d1(k).wait_send()
        fwd_d2(k).wait_send()
        send_ra(k).wait_send()
        send_rb(k).wait_send()
        y_return(k).wait_send()
        send_home(k).wait_send()
        for j in range(4):
            xq_fwd(k, j).wait_send()
        for j in (1, 2, 3):
            xt_send(k, j).wait_send()
            g_send(k, j).wait_send()
        return carry

    lax.fori_loop(0, NZ, drain, 0)


def on_device(tokens, grad_out, gates, routes, w_gate, w_up, w_down):
    dma = pltpu.SemaphoreType.DMA
    vmem = pl.BlockSpec(memory_space=pltpu.VMEM)
    anyspace = pl.BlockSpec(memory_space=pl.ANY)
    flops = 2 * 1536 * D * F * 7
    grad_tokens, grad_gate, grad_up, grad_down = pl.pallas_call(
        kernel,
        out_shape=(
            jax.ShapeDtypeStruct((T, D), BF),
            jax.ShapeDtypeStruct((QUART, F), BF),
            jax.ShapeDtypeStruct((QUART, F), BF),
            jax.ShapeDtypeStruct((F, QUART), BF),
        ),
        in_specs=[anyspace, anyspace, vmem, vmem, anyspace, anyspace, anyspace],
        out_specs=(vmem, vmem, vmem, vmem),
        scratch_shapes=[
            pltpu.VMEM((4 * T, D), BF),
            pltpu.VMEM((2, 8, T), F32),
            pltpu.VMEM((NZ, UNIT, D), BF),
            pltpu.VMEM((NZ, 4, UNIT, D), BF),
            pltpu.VMEM((D, F), BF),
            pltpu.VMEM((D, F), BF),
            pltpu.VMEM((F, D), BF),
            pltpu.VMEM((F, 32 * UNIT), BF),
            pltpu.VMEM((NZ, 4, UNIT, HALF), BF),
            pltpu.VMEM((NZ, UNIT, HALF), BF),
            pltpu.VMEM((NZ, UNIT, HALF), BF),
            pltpu.VMEM((NZ, UNIT, HALF), BF),
            pltpu.VMEM((NZ, UNIT, HALF), BF),
            pltpu.VMEM((4, F, QUART), BF),
            pltpu.VMEM((2, 128, QUART), BF),
            pltpu.VMEM((2, F, QUART), BF),
            pltpu.VMEM((2, T, D), BF),
            pltpu.VMEM((T, D), BF),
            pltpu.VMEM((2, 2 * T, NZ * UNIT), BF),
            pltpu.VMEM((NZ, UNIT, D), BF),
            pltpu.VMEM((4, 4, 2, 2, UNIT, QUART), BF),
            pltpu.VMEM((4, 4, 2, 96, 2 * F), BF),
            pltpu.VMEM((2, F, QUART), F32),
            pltpu.VMEM((NZ, 4 * UNIT, F), BF),
            dma((5,)), dma((3,)), dma((3,)),
            dma((NZ, 2)), dma((NZ, 2)), dma((NZ, 2)), dma((NZ, 2)),
            dma((NZ,)), dma((NZ,)), dma((NZ,)), dma((NZ,)),
            dma((NZ,)), dma((NZ,)), dma((NZ,)), dma((NZ,)),
            dma((NZ,)), dma((NZ,)), dma((NZ,)), dma((NZ,)),
            dma((6,)), dma((6,)), dma((2,)), dma((2,)),
            dma((NZ, 4)), dma((NZ, 4)), dma((NZ, 4)), dma((NZ, 4)), dma((NZ, 4)), dma((NZ, 4)),
        ],
        compiler_params=pltpu.CompilerParams(
            collective_id=0, has_side_effects=True, vmem_limit_bytes=62 * 1024 * 1024
        ),
        cost_estimate=pl.CostEstimate(flops=flops, bytes_accessed=10_000_000, transcendentals=0),
    )(
        tokens, grad_out, gates.reshape(1, T), routes.reshape(1, T),
        w_gate[0], w_up[0], w_down[0],
    )
    return (grad_tokens, grad_gate[None], grad_up[None], grad_down[None])


def solution(mesh):
    in_specs = (
        P(("rep", "node", "local"), None),
        P(("rep", "node", "local"), None),
        P(("rep", "node", "local"), None),
        P(("rep", "node", "local"), None),
        P(("node", "local"), None, None),
        P(("node", "local"), None, None),
        P(("node", "local"), None, None),
    )
    out_specs = (
        P(("rep", "node", "local"), None),
        P(("node", "local"), "rep", None),
        P(("node", "local"), "rep", None),
        P(("node", "local"), None, "rep"),
    )
    return jax.shard_map(
        on_device, mesh=mesh, in_specs=in_specs, out_specs=out_specs, check_vma=False
    )
```

```python
import jax
import jax.numpy as jnp
from jax import lax
from jax.experimental import pallas as pl
from jax.experimental.pallas import tpu as pltpu
from jax.sharding import PartitionSpec as P

MESH = pl.DeviceIdType.MESH
BF = jnp.bfloat16
F32 = jnp.float32

D = 3584
HALF = D // 2
QUART = D // 4
F = 256
T = 128
NZ = 8
SLOT = 24
UNIT = 2 * SLOT
NT_ROWS = (((1,), (1,)), ((), ()))


def offset_of(k):
    return ((k + 1) // 2) * (1 - 2 * ((k + 1) % 2))


def kernel(
    tok_hbm, grad_hbm, gate_ref, route_ref, wg_hbm, wu_hbm, wd_hbm,
    gt_ref, gg_ref, gu_ref, gd_ref,
    stage, meta, out, x, wg, wu, wd, at, part, rda, rdb, ry, ret, w, ar, br, fin_send, fin_recv, place,
    xt, xq, gall, acc,
    loc, ex_s, ex_r, z_s, z_r, y_s, y_r, d1_s, d1_r, d2_s, d2_r,
    ra_s, ra_r, rb_s, rb_r, ryy_s, ryy_r, h_s, h_r, rs_s, rs_r, f_s, f_r,
    xs_s, xs_r, xc_s, xc_r, gs_s, gs_r,
):
    r = lax.axis_index("rep")
    z = lax.axis_index("node")
    l = lax.axis_index("local")
    y = l // 2
    c = l % 2
    pair = y // 2
    core_peer = (r, z, y * 2 + 1 - c)
    y_peer = (r, z, (y + 1 - 2 * (y % 2)) * 2 + c)
    x_next = ((r + 1) % 4, z, l)
    x_prev = ((r + 3) % 4, z, l)
    x_far = ((r + 2) % 4, z, l)
    same = 1 - (pair + c) % 2
    far = 3 - y
    dest_l = same * (y * 2 + 1 - c) + (1 - same) * (far * 2 + c)
    src_l = (1 - same) * (y * 2 + pair) + same * (far * 2 + pair)

    def dest(k):
        return (r, (z + offset_of(k) + NZ) % NZ, dest_l)

    def source(k):
        return (r, (z - offset_of(k) + NZ) % NZ, src_l)

    def rcopy(src, dst, s, q, dev):
        return pltpu.make_async_remote_copy(
            src_ref=src, dst_ref=dst, send_sem=s, recv_sem=q, device_id=dev, device_id_type=MESH
        )

    mine = pl.ds(pl.multiple_of(c * T, T), T)
    mine_g = pl.ds(pl.multiple_of(2 * T + c * T, T), T)
    local = [
        pltpu.make_async_copy(tok_hbm, stage.at[mine], loc.at[0]),
        pltpu.make_async_copy(grad_hbm, stage.at[mine_g], loc.at[1]),
        pltpu.make_async_copy(wg_hbm, wg, loc.at[2]),
        pltpu.make_async_copy(wu_hbm, wu, loc.at[3]),
        pltpu.make_async_copy(wd_hbm, wd, loc.at[4]),
    ]
    for copy in local:
        copy.start()
    row8 = lax.broadcasted_iota(jnp.int32, (8, T), 0)
    meta[c] = jnp.where(row8 == 0, route_ref[...].astype(F32), gate_ref[...])

    barrier = pltpu.get_barrier_semaphore()
    for dev in (core_peer, y_peer, x_next, x_prev, x_far):
        pl.semaphore_signal(barrier, inc=1, device_id=dev, device_id_type=MESH)

    def greet(k, carry):
        pl.semaphore_signal(barrier, inc=1, device_id=dest(k), device_id_type=MESH)
        pl.semaphore_signal(barrier, inc=1, device_id=source(k), device_id_type=MESH)
        return carry

    lax.fori_loop(0, NZ, greet, 0)
    pl.semaphore_wait(barrier, 5 + 2 * NZ)

    exchange = [
        rcopy(meta.at[c], meta.at[c], ex_s.at[0], ex_r.at[0], core_peer),
        rcopy(tok_hbm, stage.at[mine], ex_s.at[1], ex_r.at[1], core_peer),
        rcopy(grad_hbm, stage.at[mine_g], ex_s.at[2], ex_r.at[2], core_peer),
    ]
    for copy in exchange:
        copy.start()
    exchange[0].wait_recv()
    route = jnp.concatenate([meta[0, 0:1, :], meta[1, 0:1, :]], axis=1)
    gate = jnp.concatenate([meta[0, 1:2, :], meta[1, 1:2, :]], axis=1)
    expert = lax.broadcasted_iota(jnp.int32, (16, 2 * T), 0)
    wanted = jnp.where(expert < NZ, 2 * expert + c, -1).astype(F32)
    match = jnp.where(route == wanted, 1.0, 0.0)
    earlier = lax.broadcasted_iota(jnp.int32, (2 * T, 2 * T), 0) < lax.broadcasted_iota(
        jnp.int32, (2 * T, 2 * T), 1
    )
    before = jnp.dot(
        match.astype(BF), jnp.where(earlier, 1.0, 0.0).astype(BF), preferred_element_type=F32
    )
    position = jnp.sum(before * match, axis=0, keepdims=True)
    number = jnp.sum(expert.astype(F32) * match, axis=0, keepdims=True)
    known = jnp.sum(match, axis=0, keepdims=True) > 0.5
    target = jnp.where(known, number * SLOT + position, -1.0)
    slots = lax.broadcasted_iota(jnp.int32, (NZ * SLOT, 2 * T), 0).astype(F32)
    chosen = slots == target
    slot_gate = jnp.sum(jnp.where(chosen, gate, 0.0), axis=1, keepdims=True)
    pick = jnp.where(chosen, 1.0, 0.0).astype(BF)
    local[0].wait()
    local[1].wait()
    exchange[1].wait_recv()
    exchange[2].wait_recv()

    def pack(i, carry):
        cols = pl.ds(pl.multiple_of(i * 512, 512), 512)
        rows = jnp.dot(pick, stage[0 : 2 * T, cols], preferred_element_type=F32)
        ups = jnp.dot(pick, stage[2 * T : 4 * T, cols], preferred_element_type=F32) * slot_gate
        both = jnp.concatenate(
            [rows.reshape(NZ, SLOT, 512), ups.reshape(NZ, SLOT, 512)], axis=1
        )
        out[:, :, cols] = both.astype(BF)
        return carry

    lax.fori_loop(0, D // 512, pack, 0)

    def half_cols(h):
        return pl.ds(pl.multiple_of(h * HALF, 128), HALF)

    def send_unit(k, h):
        return rcopy(
            out.at[(z + offset_of(k) + NZ) % NZ, :, half_cols(h)], x.at[k, 0, :, half_cols(h)],
            z_s.at[k, h], z_r.at[k, h], dest(k),
        )

    def fwd_y(k, h):
        return rcopy(
            x.at[k, 0, :, half_cols(h)], x.at[k, 1, :, half_cols(h)],
            y_s.at[k, h], y_r.at[k, h], y_peer,
        )

    def fwd_d1(k):
        return rcopy(x.at[k, 0], x.at[k, 2], d1_s.at[k], d1_r.at[k], core_peer)

    def fwd_d2(k):
        return rcopy(x.at[k, 1], x.at[k, 3], d2_s.at[k], d2_r.at[k], core_peer)

    def send_one(k, carry):
        send_unit(k, 0).start()
        send_unit(k, 1).start()
        return carry

    lax.fori_loop(0, NZ, send_one, 0)
    for copy in local[2:]:
        copy.wait()
    back = jnp.where(known, number * UNIT + position, -1000.0)
    unit_rows = lax.broadcasted_iota(jnp.int32, (NZ * UNIT, 2 * T), 0).astype(F32)
    for half in range(2):
        place[half] = jnp.where(unit_rows == back + half * SLOT, 1.0, 0.0).T.astype(BF)

    def forward_group(g):
        units = x.at[pl.ds(2 * g, 2)]
        rows = units[...].reshape(8 * UNIT, D)
        pre_g = jnp.dot(rows, wg[...], preferred_element_type=F32)
        pre_u = jnp.dot(rows, wu[...], preferred_element_type=F32)
        gh = lax.dot_general(rows, wd[...], NT_ROWS, preferred_element_type=F32)
        a = pre_g.reshape(8, UNIT, F)[:, :SLOT]
        u = pre_u.reshape(8, UNIT, F)[:, :SLOT]
        h = gh.reshape(8, UNIT, F)[:, SLOT:]
        sigma = 1.0 / (1.0 + jnp.exp(-a))
        swish = a * sigma
        hidden = swish * u
        d_gate = h * u * sigma * (1.0 + a * (1.0 - sigma))
        d_up = h * swish
        gall[g, 0, :, 0:F] = d_gate.reshape(192, F).astype(BF)
        gall[g, 0, :, F : 2 * F] = d_up.reshape(192, F).astype(BF)
        cols = pl.ds(pl.multiple_of(g * 384, 128), 384)
        both = jnp.concatenate([jnp.zeros_like(hidden), hidden], axis=1).reshape(8 * UNIT, F)
        at[:, cols] = both.T.astype(BF)

    def quarter(q):
        return pl.ds(pl.multiple_of(q * QUART, 128), QUART)

    def xt_send(k, j):
        return rcopy(
            xt.at[k, :, quarter((r + j) % 4)], xq.at[k // 2, 4 - j, k % 2, 0],
            xs_s.at[k, j], xs_r.at[k, 4 - j], ((r + j) % 4, z, l),
        )

    def xt_got(k, j):
        return rcopy(
            xt.at[k, :, quarter(r)], xq.at[k // 2, j, k % 2, 0],
            xs_s.at[k, j], xs_r.at[k, j], ((r + j) % 4, z, l),
        )

    def xq_fwd(k, j):
        src = xt.at[k, :, quarter(r)] if j == 0 else xq.at[k // 2, j, k % 2, 0]
        return rcopy(src, xq.at[k // 2, j, k % 2, 1], xc_s.at[k, j], xc_r.at[k, j], core_peer)

    def g_send(g, j):
        return rcopy(
            gall.at[g, 0], gall.at[g, 4 - j], gs_s.at[g, j], gs_r.at[g, 4 - j], ((r + j) % 4, z, l)
        )

    def g_got(g, j):
        return rcopy(gall.at[g, 0], gall.at[g, j], gs_s.at[g, j], gs_r.at[g, j], ((r + j) % 4, z, l))

    def compact(k):
        def columns(i, carry):
            cols = pl.ds(pl.multiple_of(i * QUART, 128), QUART)
            both = x[k, 0:2, :, cols].astype(F32)[:, :SLOT]
            xt[k, :, cols] = both.reshape(UNIT, QUART).astype(BF)
            return carry

        lax.fori_loop(0, 4, columns, 0)
        xq[k // 2, 0, k % 2, 0] = xt[k, :, quarter(r)]
        for j in (2, 1, 3):
            xt_send(k, j).start()
        xq_fwd(k, 0).start()

    def relay_quarters(g):
        for kk in range(2):
            for j in (1, 2, 3):
                xt_got(2 * g + kk, j).wait_recv()
                xq_fwd(2 * g + kk, j).start()

    def send_grads(g):
        for j in (2, 1, 3):
            g_send(g, j).start()

    def accumulate(g, first):
        for kk in range(2):
            for j in range(4):
                xq_fwd(2 * g + kk, j).wait_recv()
        for j in (1, 2, 3):
            g_got(g, j).wait_recv()
        rows = xq[g].reshape(4 * 192, QUART)
        for m in range(2):
            left = gall[g, :, :, m * F : (m + 1) * F].reshape(4 * 192, F)
            term = lax.dot_general(left, rows, (((0,), (0,)), ((), ())), preferred_element_type=F32)
            if first:
                acc[m] = term
            else:
                acc[m] += term

    def send_ra(k):
        return rcopy(part.at[k, 2], rda.at[k], ra_s.at[k], ra_r.at[k], core_peer)

    def send_rb(k):
        return rcopy(part.at[k, 3], rdb.at[k], rb_s.at[k], rb_r.at[k], core_peer)

    def route_group(g):
        left = gall[g, 0, :, 0:F]
        right = gall[g, 0, :, F : 2 * F]

        def columns(i, carry):
            done = []
            for half in range(2):
                cols = pl.ds(pl.multiple_of(half * HALF + i * 256, 256), 256)
                one = lax.dot_general(left, wg[cols, :], NT_ROWS, preferred_element_type=F32)
                one += lax.dot_general(right, wu[cols, :], NT_ROWS, preferred_element_type=F32)
                done.append(one.reshape(2, 4, SLOT, 256))
            part[pl.ds(2 * g, 2), :, :, pl.ds(pl.multiple_of(i * 256, 256), 256)] = (
                jnp.concatenate(done, axis=2).astype(BF)
            )
            return carry

        lax.fori_loop(0, HALF // 256, columns, 0)
        for kk in range(2):
            send_ra(2 * g + kk).start()
            send_rb(2 * g + kk).start()

    def y_return(k):
        return rcopy(part.at[k, 1], ry.at[k], ryy_s.at[k], ryy_r.at[k], y_peer)

    def across(k):
        send_rb(k).wait_recv()
        part[k, 1] = (part[k, 1].astype(F32) + rdb[k].astype(F32)).astype(BF)
        y_return(k).start()

    def send_home(k):
        return rcopy(part.at[k, 0], ret.at[z], h_s.at[k], h_r.at[z], source(k))

    def home(k):
        send_ra(k).wait_recv()
        y_return(k).wait_recv()
        part[k, 0] = (
            part[k, 0].astype(F32) + rda[k].astype(F32) + ry[k].astype(F32)
        ).astype(BF)
        send_home(k).start()

    def turn(t, carry):
        @pl.when(t < NZ)
        def _():
            for h in range(2):
                send_unit(t, h).wait_recv()
                fwd_y(t, h).start()
            fwd_d1(t).start()

        @pl.when(t > 0)
        def _():
            fwd_y(t - 1, 0).wait_recv()
            fwd_y(t - 1, 1).wait_recv()
            fwd_d2(t - 1).start()
            compact(t - 1)

        even = t % 2 == 0

        @pl.when(t == NZ)
        def _():
            across(5)
            across(4)
            across(3)

        @pl.when((t > 0) & even)
        def _():
            for kk in range(2):
                fwd_d1(t - 2 + kk).wait_recv()
                fwd_d2(t - 2 + kk).wait_recv()
            forward_group(t // 2 - 1)
            route_group(t // 2 - 1)

        @pl.when((t > 0) & (t < NZ) & even)
        def _():
            send_grads(t // 2 - 1)

        @pl.when((t > 2) & (t % 2 == 1))
        def _():
            relay_quarters((t - 3) // 2)

        @pl.when(t == 5)
        def _():
            accumulate(0, True)

        @pl.when(t == 7)
        def _():
            accumulate(1, False)

        return carry

    lax.fori_loop(0, NZ + 1, turn, 0)

    def weight_chunk(q):
        rows = x[:, :, :, quarter(q)].reshape(32 * UNIT, QUART)
        w[q] = jnp.dot(at[...], rows, preferred_element_type=F32).astype(BF)

    opposite, nxt, prv = (r + 2) % 4, (r + 1) % 4, (r + 3) % 4
    low, high = pl.ds(0, 128), pl.ds(128, 128)
    reduce = [
        rcopy(w.at[opposite, low], ar.at[0], rs_s.at[0], rs_r.at[0], x_next),
        rcopy(w.at[opposite, high], ar.at[1], rs_s.at[1], rs_r.at[1], x_prev),
        rcopy(w.at[nxt, high], br.at[0, high], rs_s.at[2], rs_r.at[2], x_next),
        rcopy(w.at[prv, low], br.at[1, low], rs_s.at[3], rs_r.at[3], x_prev),
        rcopy(w.at[nxt, low], br.at[0, low], rs_s.at[4], rs_r.at[4], x_next),
        rcopy(w.at[prv, high], br.at[1, high], rs_s.at[5], rs_r.at[5], x_prev),
    ]

    def step(j, carry):
        weight_chunk((r + (2 + j) * (j < 2) + (3 - j) * (j >= 2)) % 4)

        @pl.when(j == 0)
        def _():
            reduce[0].start()
            reduce[1].start()
            send_grads(3)

            def rest(m, carry):
                across((6 + m) * (m < 2) + (4 - m) * (m >= 2))
                return carry

            lax.fori_loop(0, 5, rest, 0)
            home(5)

        @pl.when(j == 1)
        def _():
            reduce[3].start()
            home(4)

        @pl.when(j == 2)
        def _():
            reduce[2].start()
            home(3)

        return carry

    lax.fori_loop(0, 4, step, 0)
    accumulate(2, False)
    home(6)
    home(7)
    relay_quarters(3)

    reduce[0].wait_recv()
    w[nxt, 0:128, :] = (w[nxt, 0:128, :].astype(F32) + ar[0].astype(F32)).astype(BF)
    reduce[4].start()
    reduce[1].wait_recv()
    w[prv, 128:256, :] = (w[prv, 128:256, :].astype(F32) + ar[1].astype(F32)).astype(BF)
    reduce[5].start()

    def near_home(m, carry):
        home(2 - m)
        return carry

    lax.fori_loop(0, 3, near_home, 0)
    accumulate(3, False)
    gg_ref[...] = acc[0].T.astype(BF)
    gu_ref[...] = acc[1].T.astype(BF)

    def arrived(j, carry):
        rcopy(part.at[j, 0], ret.at[j], h_s.at[j], h_r.at[j], source(0)).wait_recv()
        return carry

    lax.fori_loop(0, NZ, arrived, 0)

    def final(half):
        cols = pl.ds(half * HALF, HALF)
        return rcopy(
            fin_send.at[1 - c, :, cols], fin_recv.at[:, cols], f_s.at[half], f_r.at[half], core_peer
        )

    for half in range(2):

        def last(i, carry):
            cols = pl.ds(pl.multiple_of(i * 256, 256), 256)
            rows = ret[:, :, cols].reshape(NZ * UNIT, 256)
            got = jnp.dot(place[half], rows, preferred_element_type=F32)
            outc = pl.ds(pl.multiple_of(half * HALF + i * 256, 256), 256)
            fin_send[:, :, outc] = got.reshape(2, T, 256).astype(BF)
            return carry

        lax.fori_loop(0, HALF // 256, last, 0)
        final(half).start()

    for j in (2, 3, 4, 5):
        reduce[j].wait_recv()
    gd_ref[...] = (
        w[r].astype(F32) + br[0].astype(F32) + br[1].astype(F32)
    ).astype(BF)

    for half in range(2):
        final(half).wait_recv()
        cols = slice(half * HALF, (half + 1) * HALF)
        gt_ref[:, cols] = (
            fin_send[c, :, cols].astype(F32) + fin_recv[:, cols].astype(F32)
        ).astype(BF)

    for copy in exchange + reduce + [final(0), final(1)]:
        copy.wait_send()

    def drain(k, carry):
        for h in range(2):
            send_unit(k, h).wait_send()
            fwd_y(k, h).wait_send()
        fwd_d1(k).wait_send()
        fwd_d2(k).wait_send()
        send_ra(k).wait_send()
        send_rb(k).wait_send()
        y_return(k).wait_send()
        send_home(k).wait_send()
        for j in range(4):
            xq_fwd(k, j).wait_send()
        for j in (1, 2, 3):
            xt_send(k, j).wait_send()
        return carry

    lax.fori_loop(0, NZ, drain, 0)
    for g in range(4):
        for j in (1, 2, 3):
            g_send(g, j).wait_send()


def on_device(tokens, grad_out, gates, routes, w_gate, w_up, w_down):
    dma = pltpu.SemaphoreType.DMA
    vmem = pl.BlockSpec(memory_space=pltpu.VMEM)
    anyspace = pl.BlockSpec(memory_space=pl.ANY)
    flops = 2 * 1536 * D * F * 7
    grad_tokens, grad_gate, grad_up, grad_down = pl.pallas_call(
        kernel,
        out_shape=(
            jax.ShapeDtypeStruct((T, D), BF),
            jax.ShapeDtypeStruct((QUART, F), BF),
            jax.ShapeDtypeStruct((QUART, F), BF),
            jax.ShapeDtypeStruct((F, QUART), BF),
        ),
        in_specs=[anyspace, anyspace, vmem, vmem, anyspace, anyspace, anyspace],
        out_specs=(vmem, vmem, vmem, vmem),
        scratch_shapes=[
            pltpu.VMEM((4 * T, D), BF),
            pltpu.VMEM((2, 8, T), F32),
            pltpu.VMEM((NZ, UNIT, D), BF),
            pltpu.VMEM((NZ, 4, UNIT, D), BF),
            pltpu.VMEM((D, F), BF),
            pltpu.VMEM((D, F), BF),
            pltpu.VMEM((F, D), BF),
            pltpu.VMEM((F, 32 * UNIT), BF),
            pltpu.VMEM((NZ, 4, UNIT, HALF), BF),
            pltpu.VMEM((NZ, UNIT, HALF), BF),
            pltpu.VMEM((NZ, UNIT, HALF), BF),
            pltpu.VMEM((NZ, UNIT, HALF), BF),
            pltpu.VMEM((NZ, UNIT, HALF), BF),
            pltpu.VMEM((4, F, QUART), BF),
            pltpu.VMEM((2, 128, QUART), BF),
            pltpu.VMEM((2, F, QUART), BF),
            pltpu.VMEM((2, T, D), BF),
            pltpu.VMEM((T, D), BF),
            pltpu.VMEM((2, 2 * T, NZ * UNIT), BF),
            pltpu.VMEM((NZ, UNIT, D), BF),
            pltpu.VMEM((4, 4, 2, 2, UNIT, QUART), BF),
            pltpu.VMEM((4, 4, 192, 2 * F), BF),
            pltpu.VMEM((2, F, QUART), F32),
            dma((5,)), dma((3,)), dma((3,)),
            dma((NZ, 2)), dma((NZ, 2)), dma((NZ, 2)), dma((NZ, 2)),
            dma((NZ,)), dma((NZ,)), dma((NZ,)), dma((NZ,)),
            dma((NZ,)), dma((NZ,)), dma((NZ,)), dma((NZ,)),
            dma((NZ,)), dma((NZ,)), dma((NZ,)), dma((NZ,)),
            dma((6,)), dma((6,)), dma((2,)), dma((2,)),
            dma((NZ, 4)), dma((NZ, 4)), dma((NZ, 4)), dma((NZ, 4)), dma((4, 4)), dma((4, 4)),
        ],
        compiler_params=pltpu.CompilerParams(
            collective_id=0, has_side_effects=True, vmem_limit_bytes=62 * 1024 * 1024
        ),
        cost_estimate=pl.CostEstimate(flops=flops, bytes_accessed=10_000_000, transcendentals=0),
    )(
        tokens, grad_out, gates.reshape(1, T), routes.reshape(1, T),
        w_gate[0], w_up[0], w_down[0],
    )
    return (grad_tokens, grad_gate[None], grad_up[None], grad_down[None])


def solution(mesh):
    in_specs = (
        P(("rep", "node", "local"), None),
        P(("rep", "node", "local"), None),
        P(("rep", "node", "local"), None),
        P(("rep", "node", "local"), None),
        P(("node", "local"), None, None),
        P(("node", "local"), None, None),
        P(("node", "local"), None, None),
    )
    out_specs = (
        P(("rep", "node", "local"), None),
        P(("node", "local"), "rep", None),
        P(("node", "local"), "rep", None),
        P(("node", "local"), None, "rep"),
    )
    return jax.shard_map(
        on_device, mesh=mesh, in_specs=in_specs, out_specs=out_specs, check_vma=False
    )
```

```python
import jax
import jax.numpy as jnp
from jax import lax
from jax.experimental import pallas as pl
from jax.experimental.pallas import tpu as pltpu
from jax.sharding import PartitionSpec as P

MESH = pl.DeviceIdType.MESH
BF = jnp.bfloat16
F32 = jnp.float32

D = 3584
HALF = D // 2
QUART = D // 4
F = 256
T = 128
NZ = 8
SLOT = 24
UNIT = 2 * SLOT
NT_ROWS = (((1,), (1,)), ((), ()))


def offset_of(k):
    return ((k + 1) // 2) * (1 - 2 * ((k + 1) % 2))


def kernel(
    tok_hbm, grad_hbm, gate_ref, route_ref, wg_hbm, wu_hbm, wd_hbm,
    gt_ref, gg_ref, gu_ref, gd_ref,
    stage, meta, out, x, wg, wu, wd, at, part, rda, rdb, ry, ret, w, ar, br, fin_send, fin_recv, place,
    xt, xq, gall, acc,
    loc, ex_s, ex_r, z_s, z_r, y_s, y_r, d1_s, d1_r, d2_s, d2_r,
    ra_s, ra_r, rb_s, rb_r, ryy_s, ryy_r, h_s, h_r, rs_s, rs_r, f_s, f_r,
    xs_s, xs_r, xc_s, xc_r, gs_s, gs_r,
):
    r = lax.axis_index("rep")
    z = lax.axis_index("node")
    l = lax.axis_index("local")
    y = l // 2
    c = l % 2
    pair = y // 2
    core_peer = (r, z, y * 2 + 1 - c)
    y_peer = (r, z, (y + 1 - 2 * (y % 2)) * 2 + c)
    x_next = ((r + 1) % 4, z, l)
    x_prev = ((r + 3) % 4, z, l)
    x_far = ((r + 2) % 4, z, l)
    same = 1 - (pair + c) % 2
    far = 3 - y
    dest_l = same * (y * 2 + 1 - c) + (1 - same) * (far * 2 + c)
    src_l = (1 - same) * (y * 2 + pair) + same * (far * 2 + pair)

    def dest(k):
        return (r, (z + offset_of(k) + NZ) % NZ, dest_l)

    def source(k):
        return (r, (z - offset_of(k) + NZ) % NZ, src_l)

    def rcopy(src, dst, s, q, dev):
        return pltpu.make_async_remote_copy(
            src_ref=src, dst_ref=dst, send_sem=s, recv_sem=q, device_id=dev, device_id_type=MESH
        )

    mine = pl.ds(pl.multiple_of(c * T, T), T)
    mine_g = pl.ds(pl.multiple_of(2 * T + c * T, T), T)
    local = [
        pltpu.make_async_copy(tok_hbm, stage.at[mine], loc.at[0]),
        pltpu.make_async_copy(grad_hbm, stage.at[mine_g], loc.at[1]),
        pltpu.make_async_copy(wg_hbm, wg, loc.at[2]),
        pltpu.make_async_copy(wu_hbm, wu, loc.at[3]),
        pltpu.make_async_copy(wd_hbm, wd, loc.at[4]),
    ]
    for copy in local:
        copy.start()
    row8 = lax.broadcasted_iota(jnp.int32, (8, T), 0)
    meta[c] = jnp.where(row8 == 0, route_ref[...].astype(F32), gate_ref[...])

    barrier = pltpu.get_barrier_semaphore()
    for dev in (core_peer, y_peer, x_next, x_prev, x_far):
        pl.semaphore_signal(barrier, inc=1, device_id=dev, device_id_type=MESH)

    def greet(k, carry):
        pl.semaphore_signal(barrier, inc=1, device_id=dest(k), device_id_type=MESH)
        pl.semaphore_signal(barrier, inc=1, device_id=source(k), device_id_type=MESH)
        return carry

    lax.fori_loop(0, NZ, greet, 0)
    pl.semaphore_wait(barrier, 5 + 2 * NZ)

    exchange = [
        rcopy(meta.at[c], meta.at[c], ex_s.at[0], ex_r.at[0], core_peer),
        rcopy(tok_hbm, stage.at[mine], ex_s.at[1], ex_r.at[1], core_peer),
        rcopy(grad_hbm, stage.at[mine_g], ex_s.at[2], ex_r.at[2], core_peer),
    ]
    for copy in exchange:
        copy.start()
    exchange[0].wait_recv()
    route = jnp.concatenate([meta[0, 0:1, :], meta[1, 0:1, :]], axis=1)
    gate = jnp.concatenate([meta[0, 1:2, :], meta[1, 1:2, :]], axis=1)
    expert = lax.broadcasted_iota(jnp.int32, (16, 2 * T), 0)
    wanted = jnp.where(expert < NZ, 2 * expert + c, -1).astype(F32)
    match = jnp.where(route == wanted, 1.0, 0.0)
    earlier = lax.broadcasted_iota(jnp.int32, (2 * T, 2 * T), 0) < lax.broadcasted_iota(
        jnp.int32, (2 * T, 2 * T), 1
    )
    before = jnp.dot(
        match.astype(BF), jnp.where(earlier, 1.0, 0.0).astype(BF), preferred_element_type=F32
    )
    position = jnp.sum(before * match, axis=0, keepdims=True)
    number = jnp.sum(expert.astype(F32) * match, axis=0, keepdims=True)
    known = jnp.sum(match, axis=0, keepdims=True) > 0.5
    target = jnp.where(known, number * SLOT + position, -1.0)
    slots = lax.broadcasted_iota(jnp.int32, (NZ * SLOT, 2 * T), 0).astype(F32)
    chosen = slots == target
    slot_gate = jnp.sum(jnp.where(chosen, gate, 0.0), axis=1, keepdims=True)
    pick = jnp.where(chosen, 1.0, 0.0).astype(BF)
    local[0].wait()
    local[1].wait()
    exchange[1].wait_recv()
    exchange[2].wait_recv()

    def pack(i, carry):
        cols = pl.ds(pl.multiple_of(i * 512, 512), 512)
        rows = jnp.dot(pick, stage[0 : 2 * T, cols], preferred_element_type=F32)
        ups = jnp.dot(pick, stage[2 * T : 4 * T, cols], preferred_element_type=F32) * slot_gate
        both = jnp.concatenate(
            [rows.reshape(NZ, SLOT, 512), ups.reshape(NZ, SLOT, 512)], axis=1
        )
        out[:, :, cols] = both.astype(BF)
        return carry

    lax.fori_loop(0, D // 512, pack, 0)

    def half_cols(h):
        return pl.ds(pl.multiple_of(h * HALF, 128), HALF)

    def send_unit(k, h):
        return rcopy(
            out.at[(z + offset_of(k) + NZ) % NZ, :, half_cols(h)], x.at[k, 0, :, half_cols(h)],
            z_s.at[k, h], z_r.at[k, h], dest(k),
        )

    def fwd_y(k, h):
        return rcopy(
            x.at[k, 0, :, half_cols(h)], x.at[k, 1, :, half_cols(h)],
            y_s.at[k, h], y_r.at[k, h], y_peer,
        )

    def fwd_d1(k):
        return rcopy(x.at[k, 0], x.at[k, 2], d1_s.at[k], d1_r.at[k], core_peer)

    def fwd_d2(k):
        return rcopy(x.at[k, 1], x.at[k, 3], d2_s.at[k], d2_r.at[k], core_peer)

    def send_one(k, carry):
        send_unit(k, 0).start()
        send_unit(k, 1).start()
        return carry

    lax.fori_loop(0, NZ, send_one, 0)
    for copy in local[2:]:
        copy.wait()
    back = jnp.where(known, number * UNIT + position, -1000.0)
    unit_rows = lax.broadcasted_iota(jnp.int32, (NZ * UNIT, 2 * T), 0).astype(F32)
    for half in range(2):
        place[half] = jnp.where(unit_rows == back + half * SLOT, 1.0, 0.0).T.astype(BF)

    def forward_group(g):
        units = x.at[pl.ds(2 * g, 2)]
        rows = units[...].reshape(8 * UNIT, D)
        pre_g = jnp.dot(rows, wg[...], preferred_element_type=F32)
        pre_u = jnp.dot(rows, wu[...], preferred_element_type=F32)
        gh = lax.dot_general(rows, wd[...], NT_ROWS, preferred_element_type=F32)
        a = pre_g.reshape(8, UNIT, F)[:, :SLOT]
        u = pre_u.reshape(8, UNIT, F)[:, :SLOT]
        h = gh.reshape(8, UNIT, F)[:, SLOT:]
        sigma = 1.0 / (1.0 + jnp.exp(-a))
        swish = a * sigma
        hidden = swish * u
        d_gate = h * u * sigma * (1.0 + a * (1.0 - sigma))
        d_up = h * swish
        gall[g, 0, :, 0:F] = d_gate.reshape(192, F).astype(BF)
        gall[g, 0, :, F : 2 * F] = d_up.reshape(192, F).astype(BF)
        cols = pl.ds(pl.multiple_of(g * 384, 128), 384)
        both = jnp.concatenate([jnp.zeros_like(hidden), hidden], axis=1).reshape(8 * UNIT, F)
        at[:, cols] = both.T.astype(BF)

    def quarter(q):
        return pl.ds(pl.multiple_of(q * QUART, 128), QUART)

    def xt_send(k, j):
        return rcopy(
            xt.at[k, :, quarter((r + j) % 4)], xq.at[k // 2, 4 - j, k % 2, 0],
            xs_s.at[k, j], xs_r.at[k, 4 - j], ((r + j) % 4, z, l),
        )

    def xt_got(k, j):
        return rcopy(
            xt.at[k, :, quarter(r)], xq.at[k // 2, j, k % 2, 0],
            xs_s.at[k, j], xs_r.at[k, j], ((r + j) % 4, z, l),
        )

    def xq_fwd(k, j):
        src = xt.at[k, :, quarter(r)] if j == 0 else xq.at[k // 2, j, k % 2, 0]
        return rcopy(src, xq.at[k // 2, j, k % 2, 1], xc_s.at[k, j], xc_r.at[k, j], core_peer)

    def g_send(g, j):
        return rcopy(
            gall.at[g, 0], gall.at[g, 4 - j], gs_s.at[g, j], gs_r.at[g, 4 - j], ((r + j) % 4, z, l)
        )

    def g_got(g, j):
        return rcopy(gall.at[g, 0], gall.at[g, j], gs_s.at[g, j], gs_r.at[g, j], ((r + j) % 4, z, l))

    def compact(k):
        def columns(i, carry):
            cols = pl.ds(pl.multiple_of(i * QUART, 128), QUART)
            both = x[k, 0:2, :, cols].astype(F32)[:, :SLOT]
            xt[k, :, cols] = both.reshape(UNIT, QUART).astype(BF)
            return carry

        lax.fori_loop(0, 4, columns, 0)
        xq[k // 2, 0, k % 2, 0] = xt[k, :, quarter(r)]
        for j in (2, 1, 3):
            xt_send(k, j).start()
        xq_fwd(k, 0).start()

    def relay_quarters(g):
        for kk in range(2):
            for j in (1, 2, 3):
                xt_got(2 * g + kk, j).wait_recv()
                xq_fwd(2 * g + kk, j).start()

    def send_grads(g):
        for j in (2, 1, 3):
            g_send(g, j).start()

    def accumulate(g, first):
        for kk in range(2):
            for j in range(4):
                xq_fwd(2 * g + kk, j).wait_recv()
        for j in (1, 2, 3):
            g_got(g, j).wait_recv()
        rows = xq[g].reshape(4 * 192, QUART)
        for m in range(2):
            left = gall[g, :, :, m * F : (m + 1) * F].reshape(4 * 192, F)
            term = lax.dot_general(left, rows, (((0,), (0,)), ((), ())), preferred_element_type=F32)
            if first:
                acc[m] = term
            else:
                acc[m] += term

    def send_ra(k):
        return rcopy(part.at[k, 2], rda.at[k], ra_s.at[k], ra_r.at[k], core_peer)

    def send_rb(k):
        return rcopy(part.at[k, 3], rdb.at[k], rb_s.at[k], rb_r.at[k], core_peer)

    def route_group(g):
        left = gall[g, 0, :, 0:F]
        right = gall[g, 0, :, F : 2 * F]

        def columns(i, carry):
            done = []
            for half in range(2):
                cols = pl.ds(pl.multiple_of(half * HALF + i * 256, 256), 256)
                one = lax.dot_general(left, wg[cols, :], NT_ROWS, preferred_element_type=F32)
                one += lax.dot_general(right, wu[cols, :], NT_ROWS, preferred_element_type=F32)
                done.append(one.reshape(2, 4, SLOT, 256))
            part[pl.ds(2 * g, 2), :, :, pl.ds(pl.multiple_of(i * 256, 256), 256)] = (
                jnp.concatenate(done, axis=2).astype(BF)
            )
            return carry

        lax.fori_loop(0, HALF // 256, columns, 0)
        for kk in range(2):
            send_ra(2 * g + kk).start()
            send_rb(2 * g + kk).start()

    def y_return(k):
        return rcopy(part.at[k, 1], ry.at[k], ryy_s.at[k], ryy_r.at[k], y_peer)

    def across(k):
        send_rb(k).wait_recv()
        part[k, 1] = (part[k, 1].astype(F32) + rdb[k].astype(F32)).astype(BF)
        y_return(k).start()

    def send_home(k):
        return rcopy(part.at[k, 0], ret.at[z], h_s.at[k], h_r.at[z], source(k))

    def home(k):
        send_ra(k).wait_recv()
        y_return(k).wait_recv()
        part[k, 0] = (
            part[k, 0].astype(F32) + rda[k].astype(F32) + ry[k].astype(F32)
        ).astype(BF)
        send_home(k).start()

    def relay(k):
        for h in range(2):
            send_unit(k, h).wait_recv()
            fwd_y(k, h).start()
        fwd_d1(k).start()

    def turn(t, carry):
        @pl.when(t < NZ - 1)
        def _():
            relay(t)

        @pl.when(t > 0)
        def _():
            fwd_y(t - 1, 0).wait_recv()
            fwd_y(t - 1, 1).wait_recv()
            fwd_d2(t - 1).start()
            compact(t - 1)

        @pl.when(t == NZ - 1)
        def _():
            across(5)
            across(4)
            relay(NZ - 1)

        even = t % 2 == 0

        @pl.when(t == NZ)
        def _():
            home(5)
            home(4)
            across(3)
            across(2)

        @pl.when((t > 0) & even)
        def _():
            for kk in range(2):
                fwd_d1(t - 2 + kk).wait_recv()
                fwd_d2(t - 2 + kk).wait_recv()
            forward_group(t // 2 - 1)
            route_group(t // 2 - 1)

        @pl.when((t > 0) & (t < NZ) & even)
        def _():
            send_grads(t // 2 - 1)

        @pl.when((t > 2) & (t % 2 == 1))
        def _():
            relay_quarters((t - 3) // 2)

        @pl.when(t == 5)
        def _():
            accumulate(0, True)

        @pl.when(t == 7)
        def _():
            accumulate(1, False)

        return carry

    lax.fori_loop(0, NZ + 1, turn, 0)

    def weight_chunk(q):
        rows = x[:, :, :, quarter(q)].reshape(32 * UNIT, QUART)
        w[q] = jnp.dot(at[...], rows, preferred_element_type=F32).astype(BF)

    opposite, nxt, prv = (r + 2) % 4, (r + 1) % 4, (r + 3) % 4
    low, high = pl.ds(0, 128), pl.ds(128, 128)
    reduce = [
        rcopy(w.at[opposite, low], ar.at[0], rs_s.at[0], rs_r.at[0], x_next),
        rcopy(w.at[opposite, high], ar.at[1], rs_s.at[1], rs_r.at[1], x_prev),
        rcopy(w.at[nxt, high], br.at[0, high], rs_s.at[2], rs_r.at[2], x_next),
        rcopy(w.at[prv, low], br.at[1, low], rs_s.at[3], rs_r.at[3], x_prev),
        rcopy(w.at[nxt, low], br.at[0, low], rs_s.at[4], rs_r.at[4], x_next),
        rcopy(w.at[prv, high], br.at[1, high], rs_s.at[5], rs_r.at[5], x_prev),
    ]

    def step(j, carry):
        weight_chunk((r + (2 + j) * (j < 2) + (3 - j) * (j >= 2)) % 4)

        @pl.when(j == 0)
        def _():
            reduce[0].start()
            reduce[1].start()
            send_grads(3)

            def rest(m, carry):
                across((6 + m) * (m < 2) + (3 - m) * (m >= 2))
                return carry

            lax.fori_loop(0, 4, rest, 0)
            home(3)

        @pl.when(j == 1)
        def _():
            reduce[3].start()
            home(2)

        @pl.when(j == 2)
        def _():
            reduce[2].start()

        return carry

    lax.fori_loop(0, 4, step, 0)
    accumulate(2, False)
    home(6)
    home(7)
    relay_quarters(3)

    reduce[0].wait_recv()
    w[nxt, 0:128, :] = (w[nxt, 0:128, :].astype(F32) + ar[0].astype(F32)).astype(BF)
    reduce[4].start()
    reduce[1].wait_recv()
    w[prv, 128:256, :] = (w[prv, 128:256, :].astype(F32) + ar[1].astype(F32)).astype(BF)
    reduce[5].start()

    def near_home(m, carry):
        home(1 - m)
        return carry

    lax.fori_loop(0, 2, near_home, 0)
    accumulate(3, False)
    gg_ref[...] = acc[0].T.astype(BF)
    gu_ref[...] = acc[1].T.astype(BF)

    def arrived(j, carry):
        rcopy(part.at[j, 0], ret.at[j], h_s.at[j], h_r.at[j], source(0)).wait_recv()
        return carry

    lax.fori_loop(0, NZ, arrived, 0)

    def final(half):
        cols = pl.ds(half * HALF, HALF)
        return rcopy(
            fin_send.at[1 - c, :, cols], fin_recv.at[:, cols], f_s.at[half], f_r.at[half], core_peer
        )

    for half in range(2):

        def last(i, carry):
            cols = pl.ds(pl.multiple_of(i * 256, 256), 256)
            rows = ret[:, :, cols].reshape(NZ * UNIT, 256)
            got = jnp.dot(place[half], rows, preferred_element_type=F32)
            outc = pl.ds(pl.multiple_of(half * HALF + i * 256, 256), 256)
            fin_send[:, :, outc] = got.reshape(2, T, 256).astype(BF)
            return carry

        lax.fori_loop(0, HALF // 256, last, 0)
        final(half).start()

    for j in (2, 3, 4, 5):
        reduce[j].wait_recv()
    gd_ref[...] = (
        w[r].astype(F32) + br[0].astype(F32) + br[1].astype(F32)
    ).astype(BF)

    for half in range(2):
        final(half).wait_recv()
        cols = slice(half * HALF, (half + 1) * HALF)
        gt_ref[:, cols] = (
            fin_send[c, :, cols].astype(F32) + fin_recv[:, cols].astype(F32)
        ).astype(BF)

    for copy in exchange + reduce + [final(0), final(1)]:
        copy.wait_send()

    def drain(k, carry):
        for h in range(2):
            send_unit(k, h).wait_send()
            fwd_y(k, h).wait_send()
        fwd_d1(k).wait_send()
        fwd_d2(k).wait_send()
        send_ra(k).wait_send()
        send_rb(k).wait_send()
        y_return(k).wait_send()
        send_home(k).wait_send()
        for j in range(4):
            xq_fwd(k, j).wait_send()
        for j in (1, 2, 3):
            xt_send(k, j).wait_send()
        return carry

    lax.fori_loop(0, NZ, drain, 0)
    for g in range(4):
        for j in (1, 2, 3):
            g_send(g, j).wait_send()


def on_device(tokens, grad_out, gates, routes, w_gate, w_up, w_down):
    dma = pltpu.SemaphoreType.DMA
    vmem = pl.BlockSpec(memory_space=pltpu.VMEM)
    anyspace = pl.BlockSpec(memory_space=pl.ANY)
    flops = 2 * 1536 * D * F * 7
    grad_tokens, grad_gate, grad_up, grad_down = pl.pallas_call(
        kernel,
        out_shape=(
            jax.ShapeDtypeStruct((T, D), BF),
            jax.ShapeDtypeStruct((QUART, F), BF),
            jax.ShapeDtypeStruct((QUART, F), BF),
            jax.ShapeDtypeStruct((F, QUART), BF),
        ),
        in_specs=[anyspace, anyspace, vmem, vmem, anyspace, anyspace, anyspace],
        out_specs=(vmem, vmem, vmem, vmem),
        scratch_shapes=[
            pltpu.VMEM((4 * T, D), BF),
            pltpu.VMEM((2, 8, T), F32),
            pltpu.VMEM((NZ, UNIT, D), BF),
            pltpu.VMEM((NZ, 4, UNIT, D), BF),
            pltpu.VMEM((D, F), BF),
            pltpu.VMEM((D, F), BF),
            pltpu.VMEM((F, D), BF),
            pltpu.VMEM((F, 32 * UNIT), BF),
            pltpu.VMEM((NZ, 4, UNIT, HALF), BF),
            pltpu.VMEM((NZ, UNIT, HALF), BF),
            pltpu.VMEM((NZ, UNIT, HALF), BF),
            pltpu.VMEM((NZ, UNIT, HALF), BF),
            pltpu.VMEM((NZ, UNIT, HALF), BF),
            pltpu.VMEM((4, F, QUART), BF),
            pltpu.VMEM((2, 128, QUART), BF),
            pltpu.VMEM((2, F, QUART), BF),
            pltpu.VMEM((2, T, D), BF),
            pltpu.VMEM((T, D), BF),
            pltpu.VMEM((2, 2 * T, NZ * UNIT), BF),
            pltpu.VMEM((NZ, UNIT, D), BF),
            pltpu.VMEM((4, 4, 2, 2, UNIT, QUART), BF),
            pltpu.VMEM((4, 4, 192, 2 * F), BF),
            pltpu.VMEM((2, F, QUART), F32),
            dma((5,)), dma((3,)), dma((3,)),
            dma((NZ, 2)), dma((NZ, 2)), dma((NZ, 2)), dma((NZ, 2)),
            dma((NZ,)), dma((NZ,)), dma((NZ,)), dma((NZ,)),
            dma((NZ,)), dma((NZ,)), dma((NZ,)), dma((NZ,)),
            dma((NZ,)), dma((NZ,)), dma((NZ,)), dma((NZ,)),
            dma((6,)), dma((6,)), dma((2,)), dma((2,)),
            dma((NZ, 4)), dma((NZ, 4)), dma((NZ, 4)), dma((NZ, 4)), dma((4, 4)), dma((4, 4)),
        ],
        compiler_params=pltpu.CompilerParams(
            collective_id=0, has_side_effects=True, vmem_limit_bytes=62 * 1024 * 1024
        ),
        cost_estimate=pl.CostEstimate(flops=flops, bytes_accessed=10_000_000, transcendentals=0),
    )(
        tokens, grad_out, gates.reshape(1, T), routes.reshape(1, T),
        w_gate[0], w_up[0], w_down[0],
    )
    return (grad_tokens, grad_gate[None], grad_up[None], grad_down[None])


def solution(mesh):
    in_specs = (
        P(("rep", "node", "local"), None),
        P(("rep", "node", "local"), None),
        P(("rep", "node", "local"), None),
        P(("rep", "node", "local"), None),
        P(("node", "local"), None, None),
        P(("node", "local"), None, None),
        P(("node", "local"), None, None),
    )
    out_specs = (
        P(("rep", "node", "local"), None),
        P(("node", "local"), "rep", None),
        P(("node", "local"), "rep", None),
        P(("node", "local"), None, "rep"),
    )
    return jax.shard_map(
        on_device, mesh=mesh, in_specs=in_specs, out_specs=out_specs, check_vma=False
    )
```

```python
import jax
import jax.numpy as jnp
from jax import lax
from jax.experimental import pallas as pl
from jax.experimental.pallas import tpu as pltpu
from jax.sharding import PartitionSpec as P

MESH = pl.DeviceIdType.MESH
BF = jnp.bfloat16
F32 = jnp.float32

D = 3584
HALF = D // 2
QUART = D // 4
F = 256
T = 128
NZ = 8
SLOT = 24
UNIT = 2 * SLOT
NT_ROWS = (((1,), (1,)), ((), ()))


def offset_of(k):
    return ((k + 1) // 2) * (1 - 2 * ((k + 1) % 2))


def kernel(
    tok_hbm, grad_hbm, gate_ref, route_ref, wg_hbm, wu_hbm, wd_hbm,
    gt_ref, gg_ref, gu_ref, gd_ref,
    stage, meta, out, x, wg, wu, wd, at, part, rda, rdb, ry, ret, w, ar, br, fin_send, fin_recv, place,
    xt, xq, gall, acc,
    loc, ex_s, ex_r, z_s, z_r, y_s, y_r, d1_s, d1_r, d2_s, d2_r,
    ra_s, ra_r, rb_s, rb_r, ryy_s, ryy_r, h_s, h_r, rs_s, rs_r, f_s, f_r,
    xs_s, xs_r, xc_s, xc_r, gs_s, gs_r,
):
    r = lax.axis_index("rep")
    z = lax.axis_index("node")
    l = lax.axis_index("local")
    y = l // 2
    c = l % 2
    pair = y // 2
    core_peer = (r, z, y * 2 + 1 - c)
    y_peer = (r, z, (y + 1 - 2 * (y % 2)) * 2 + c)
    x_next = ((r + 1) % 4, z, l)
    x_prev = ((r + 3) % 4, z, l)
    x_far = ((r + 2) % 4, z, l)
    same = 1 - (pair + c) % 2
    far = 3 - y
    dest_l = same * (y * 2 + 1 - c) + (1 - same) * (far * 2 + c)
    src_l = (1 - same) * (y * 2 + pair) + same * (far * 2 + pair)

    def dest(k):
        return (r, (z + offset_of(k) + NZ) % NZ, dest_l)

    def source(k):
        return (r, (z - offset_of(k) + NZ) % NZ, src_l)

    def rcopy(src, dst, s, q, dev):
        return pltpu.make_async_remote_copy(
            src_ref=src, dst_ref=dst, send_sem=s, recv_sem=q, device_id=dev, device_id_type=MESH
        )

    mine = pl.ds(pl.multiple_of(c * T, T), T)
    mine_g = pl.ds(pl.multiple_of(2 * T + c * T, T), T)
    local = [
        pltpu.make_async_copy(tok_hbm, stage.at[mine], loc.at[0]),
        pltpu.make_async_copy(grad_hbm, stage.at[mine_g], loc.at[1]),
        pltpu.make_async_copy(wg_hbm, wg, loc.at[2]),
        pltpu.make_async_copy(wu_hbm, wu, loc.at[3]),
        pltpu.make_async_copy(wd_hbm, wd, loc.at[4]),
    ]
    for copy in local:
        copy.start()
    row8 = lax.broadcasted_iota(jnp.int32, (8, T), 0)
    meta[c] = jnp.where(row8 == 0, route_ref[...].astype(F32), gate_ref[...])

    barrier = pltpu.get_barrier_semaphore()
    for dev in (core_peer, y_peer, x_next, x_prev, x_far):
        pl.semaphore_signal(barrier, inc=1, device_id=dev, device_id_type=MESH)

    def greet(k, carry):
        pl.semaphore_signal(barrier, inc=1, device_id=dest(k), device_id_type=MESH)
        pl.semaphore_signal(barrier, inc=1, device_id=source(k), device_id_type=MESH)
        return carry

    lax.fori_loop(0, NZ, greet, 0)
    pl.semaphore_wait(barrier, 5 + 2 * NZ)

    exchange = [
        rcopy(meta.at[c], meta.at[c], ex_s.at[0], ex_r.at[0], core_peer),
        rcopy(tok_hbm, stage.at[mine], ex_s.at[1], ex_r.at[1], core_peer),
        rcopy(grad_hbm, stage.at[mine_g], ex_s.at[2], ex_r.at[2], core_peer),
    ]
    for copy in exchange:
        copy.start()
    exchange[0].wait_recv()
    route = jnp.concatenate([meta[0, 0:1, :], meta[1, 0:1, :]], axis=1)
    gate = jnp.concatenate([meta[0, 1:2, :], meta[1, 1:2, :]], axis=1)
    expert = lax.broadcasted_iota(jnp.int32, (16, 2 * T), 0)
    wanted = jnp.where(expert < NZ, 2 * expert + c, -1).astype(F32)
    match = jnp.where(route == wanted, 1.0, 0.0)
    earlier = lax.broadcasted_iota(jnp.int32, (2 * T, 2 * T), 0) < lax.broadcasted_iota(
        jnp.int32, (2 * T, 2 * T), 1
    )
    before = jnp.dot(
        match.astype(BF), jnp.where(earlier, 1.0, 0.0).astype(BF), preferred_element_type=F32
    )
    position = jnp.sum(before * match, axis=0, keepdims=True)
    number = jnp.sum(expert.astype(F32) * match, axis=0, keepdims=True)
    known = jnp.sum(match, axis=0, keepdims=True) > 0.5
    target = jnp.where(known, number * SLOT + position, -1.0)
    slots = lax.broadcasted_iota(jnp.int32, (NZ * SLOT, 2 * T), 0).astype(F32)
    chosen = slots == target
    slot_gate = jnp.sum(jnp.where(chosen, gate, 0.0), axis=1, keepdims=True)
    pick = jnp.where(chosen, 1.0, 0.0).astype(BF)
    local[0].wait()
    local[1].wait()
    exchange[1].wait_recv()
    exchange[2].wait_recv()

    def pack(i, carry):
        cols = pl.ds(pl.multiple_of(i * 512, 512), 512)
        rows = jnp.dot(pick, stage[0 : 2 * T, cols], preferred_element_type=F32)
        ups = jnp.dot(pick, stage[2 * T : 4 * T, cols], preferred_element_type=F32) * slot_gate
        both = jnp.concatenate(
            [rows.reshape(NZ, SLOT, 512), ups.reshape(NZ, SLOT, 512)], axis=1
        )
        out[:, :, cols] = both.astype(BF)
        return carry

    lax.fori_loop(0, D // 512, pack, 0)

    def half_cols(h):
        return pl.ds(pl.multiple_of(h * HALF, 128), HALF)

    def send_unit(k, h):
        return rcopy(
            out.at[(z + offset_of(k) + NZ) % NZ, :, half_cols(h)], x.at[k, 0, :, half_cols(h)],
            z_s.at[k, h], z_r.at[k, h], dest(k),
        )

    def fwd_y(k, h):
        return rcopy(
            x.at[k, 0, :, half_cols(h)], x.at[k, 1, :, half_cols(h)],
            y_s.at[k, h], y_r.at[k, h], y_peer,
        )

    def fwd_d1(k):
        return rcopy(x.at[k, 0], x.at[k, 2], d1_s.at[k], d1_r.at[k], core_peer)

    def fwd_d2(k):
        return rcopy(x.at[k, 1], x.at[k, 3], d2_s.at[k], d2_r.at[k], core_peer)

    def send_one(k, carry):
        send_unit(k, 0).start()
        send_unit(k, 1).start()
        return carry

    lax.fori_loop(0, 5, send_one, 0)
    for copy in local[2:]:
        copy.wait()
    back = jnp.where(known, number * UNIT + position, -1000.0)
    unit_rows = lax.broadcasted_iota(jnp.int32, (NZ * UNIT, 2 * T), 0).astype(F32)
    for half in range(2):
        place[half] = jnp.where(unit_rows == back + half * SLOT, 1.0, 0.0).T.astype(BF)

    def forward_group(g):
        units = x.at[pl.ds(2 * g, 2)]
        rows = units[...].reshape(8 * UNIT, D)
        pre_g = jnp.dot(rows, wg[...], preferred_element_type=F32)
        pre_u = jnp.dot(rows, wu[...], preferred_element_type=F32)
        gh = lax.dot_general(rows, wd[...], NT_ROWS, preferred_element_type=F32)
        a = pre_g.reshape(8, UNIT, F)[:, :SLOT]
        u = pre_u.reshape(8, UNIT, F)[:, :SLOT]
        h = gh.reshape(8, UNIT, F)[:, SLOT:]
        sigma = 1.0 / (1.0 + jnp.exp(-a))
        swish = a * sigma
        hidden = swish * u
        d_gate = h * u * sigma * (1.0 + a * (1.0 - sigma))
        d_up = h * swish
        gall[g, 0, :, 0:F] = d_gate.reshape(192, F).astype(BF)
        gall[g, 0, :, F : 2 * F] = d_up.reshape(192, F).astype(BF)
        cols = pl.ds(pl.multiple_of(g * 384, 128), 384)
        both = jnp.concatenate([jnp.zeros_like(hidden), hidden], axis=1).reshape(8 * UNIT, F)
        at[:, cols] = both.T.astype(BF)

    def quarter(q):
        return pl.ds(pl.multiple_of(q * QUART, 128), QUART)

    def xt_send(k, j):
        return rcopy(
            xt.at[k, :, quarter((r + j) % 4)], xq.at[k // 2, 4 - j, k % 2, 0],
            xs_s.at[k, j], xs_r.at[k, 4 - j], ((r + j) % 4, z, l),
        )

    def xt_got(k, j):
        return rcopy(
            xt.at[k, :, quarter(r)], xq.at[k // 2, j, k % 2, 0],
            xs_s.at[k, j], xs_r.at[k, j], ((r + j) % 4, z, l),
        )

    def xq_fwd(k, j):
        src = xt.at[k, :, quarter(r)] if j == 0 else xq.at[k // 2, j, k % 2, 0]
        return rcopy(src, xq.at[k // 2, j, k % 2, 1], xc_s.at[k, j], xc_r.at[k, j], core_peer)

    def g_send(g, j):
        return rcopy(
            gall.at[g, 0], gall.at[g, 4 - j], gs_s.at[g, j], gs_r.at[g, 4 - j], ((r + j) % 4, z, l)
        )

    def g_got(g, j):
        return rcopy(gall.at[g, 0], gall.at[g, j], gs_s.at[g, j], gs_r.at[g, j], ((r + j) % 4, z, l))

    def compact(k):
        def columns(i, carry):
            cols = pl.ds(pl.multiple_of(i * QUART, 128), QUART)
            both = x[k, 0:2, :, cols].astype(F32)[:, :SLOT]
            xt[k, :, cols] = both.reshape(UNIT, QUART).astype(BF)
            return carry

        lax.fori_loop(0, 4, columns, 0)
        xq[k // 2, 0, k % 2, 0] = xt[k, :, quarter(r)]
        for j in (2, 1, 3):
            xt_send(k, j).start()
        xq_fwd(k, 0).start()

    def relay_quarters(g):
        for kk in range(2):
            for j in (1, 2, 3):
                xt_got(2 * g + kk, j).wait_recv()
                xq_fwd(2 * g + kk, j).start()

    def send_grads(g):
        for j in (2, 1, 3):
            g_send(g, j).start()

    def accumulate(g, first):
        for kk in range(2):
            for j in range(4):
                xq_fwd(2 * g + kk, j).wait_recv()
        for j in (1, 2, 3):
            g_got(g, j).wait_recv()
        rows = xq[g].reshape(4 * 192, QUART)
        for m in range(2):
            left = gall[g, :, :, m * F : (m + 1) * F].reshape(4 * 192, F)
            term = lax.dot_general(left, rows, (((0,), (0,)), ((), ())), preferred_element_type=F32)
            if first:
                acc[m] = term
            else:
                acc[m] += term

    def send_ra(k):
        return rcopy(part.at[k, 2], rda.at[k], ra_s.at[k], ra_r.at[k], core_peer)

    def send_rb(k):
        return rcopy(part.at[k, 3], rdb.at[k], rb_s.at[k], rb_r.at[k], core_peer)

    def route_group(g):
        left = gall[g, 0, :, 0:F]
        right = gall[g, 0, :, F : 2 * F]

        def columns(i, carry):
            done = []
            for half in range(2):
                cols = pl.ds(pl.multiple_of(half * HALF + i * 256, 256), 256)
                one = lax.dot_general(left, wg[cols, :], NT_ROWS, preferred_element_type=F32)
                one += lax.dot_general(right, wu[cols, :], NT_ROWS, preferred_element_type=F32)
                done.append(one.reshape(2, 4, SLOT, 256))
            part[pl.ds(2 * g, 2), :, :, pl.ds(pl.multiple_of(i * 256, 256), 256)] = (
                jnp.concatenate(done, axis=2).astype(BF)
            )
            return carry

        lax.fori_loop(0, HALF // 256, columns, 0)
        for kk in range(2):
            send_ra(2 * g + kk).start()
            send_rb(2 * g + kk).start()

    def y_return(k):
        return rcopy(part.at[k, 1], ry.at[k], ryy_s.at[k], ryy_r.at[k], y_peer)

    def across(k):
        send_rb(k).wait_recv()
        part[k, 1] = (part[k, 1].astype(F32) + rdb[k].astype(F32)).astype(BF)
        y_return(k).start()

    def send_home(k):
        return rcopy(part.at[k, 0], ret.at[z], h_s.at[k], h_r.at[z], source(k))

    def home(k):
        send_ra(k).wait_recv()
        y_return(k).wait_recv()
        part[k, 0] = (
            part[k, 0].astype(F32) + rda[k].astype(F32) + ry[k].astype(F32)
        ).astype(BF)
        send_home(k).start()

    def turn(t, carry):
        @pl.when(t < NZ)
        def _():
            for h in range(2):
                send_unit(t, h).wait_recv()
                fwd_y(t, h).start()
            fwd_d1(t).start()

        @pl.when((t > 0) & (t < 4))
        def _():
            send_unit(t + 4, 0).start()
            send_unit(t + 4, 1).start()

        @pl.when(t > 0)
        def _():
            fwd_y(t - 1, 0).wait_recv()
            fwd_y(t - 1, 1).wait_recv()
            fwd_d2(t - 1).start()
            compact(t - 1)

        even = t % 2 == 0

        @pl.when(t == NZ)
        def _():
            across(5)
            across(4)
            across(3)

        @pl.when((t > 0) & even)
        def _():
            for kk in range(2):
                fwd_d1(t - 2 + kk).wait_recv()
                fwd_d2(t - 2 + kk).wait_recv()
            forward_group(t // 2 - 1)
            route_group(t // 2 - 1)

        @pl.when((t > 0) & (t < NZ) & even)
        def _():
            send_grads(t // 2 - 1)

        @pl.when((t > 2) & (t % 2 == 1))
        def _():
            relay_quarters((t - 3) // 2)

        @pl.when(t == 5)
        def _():
            accumulate(0, True)

        @pl.when(t == 7)
        def _():
            accumulate(1, False)

        return carry

    lax.fori_loop(0, NZ + 1, turn, 0)

    def weight_chunk(q):
        rows = x[:, :, :, quarter(q)].reshape(32 * UNIT, QUART)
        w[q] = jnp.dot(at[...], rows, preferred_element_type=F32).astype(BF)

    opposite, nxt, prv = (r + 2) % 4, (r + 1) % 4, (r + 3) % 4
    low, high = pl.ds(0, 128), pl.ds(128, 128)
    reduce = [
        rcopy(w.at[opposite, low], ar.at[0], rs_s.at[0], rs_r.at[0], x_next),
        rcopy(w.at[opposite, high], ar.at[1], rs_s.at[1], rs_r.at[1], x_prev),
        rcopy(w.at[nxt, high], br.at[0, high], rs_s.at[2], rs_r.at[2], x_next),
        rcopy(w.at[prv, low], br.at[1, low], rs_s.at[3], rs_r.at[3], x_prev),
        rcopy(w.at[nxt, low], br.at[0, low], rs_s.at[4], rs_r.at[4], x_next),
        rcopy(w.at[prv, high], br.at[1, high], rs_s.at[5], rs_r.at[5], x_prev),
    ]

    def step(j, carry):
        weight_chunk((r + (2 + j) * (j < 2) + (3 - j) * (j >= 2)) % 4)

        @pl.when(j == 0)
        def _():
            reduce[0].start()
            reduce[1].start()
            send_grads(3)

            def rest(m, carry):
                across((6 + m) * (m < 2) + (4 - m) * (m >= 2))
                return carry

            lax.fori_loop(0, 5, rest, 0)
            home(5)

        @pl.when(j == 1)
        def _():
            reduce[3].start()
            home(4)

        @pl.when(j == 2)
        def _():
            reduce[2].start()
            home(3)

        return carry

    lax.fori_loop(0, 4, step, 0)
    accumulate(2, False)
    home(6)
    home(7)
    relay_quarters(3)

    reduce[0].wait_recv()
    w[nxt, 0:128, :] = (w[nxt, 0:128, :].astype(F32) + ar[0].astype(F32)).astype(BF)
    reduce[4].start()
    reduce[1].wait_recv()
    w[prv, 128:256, :] = (w[prv, 128:256, :].astype(F32) + ar[1].astype(F32)).astype(BF)
    reduce[5].start()

    def near_home(m, carry):
        home(2 - m)
        return carry

    lax.fori_loop(0, 3, near_home, 0)
    accumulate(3, False)
    gg_ref[...] = acc[0].T.astype(BF)
    gu_ref[...] = acc[1].T.astype(BF)

    def arrived(j, carry):
        rcopy(part.at[j, 0], ret.at[j], h_s.at[j], h_r.at[j], source(0)).wait_recv()
        return carry

    lax.fori_loop(0, NZ, arrived, 0)

    def final(half):
        cols = pl.ds(half * HALF, HALF)
        return rcopy(
            fin_send.at[1 - c, :, cols], fin_recv.at[:, cols], f_s.at[half], f_r.at[half], core_peer
        )

    for half in range(2):

        def last(i, carry):
            cols = pl.ds(pl.multiple_of(i * 256, 256), 256)
            rows = ret[:, :, cols].reshape(NZ * UNIT, 256)
            got = jnp.dot(place[half], rows, preferred_element_type=F32)
            outc = pl.ds(pl.multiple_of(half * HALF + i * 256, 256), 256)
            fin_send[:, :, outc] = got.reshape(2, T, 256).astype(BF)
            return carry

        lax.fori_loop(0, HALF // 256, last, 0)
        final(half).start()

    for j in (2, 3, 4, 5):
        reduce[j].wait_recv()
    gd_ref[...] = (
        w[r].astype(F32) + br[0].astype(F32) + br[1].astype(F32)
    ).astype(BF)

    for half in range(2):
        final(half).wait_recv()
        cols = slice(half * HALF, (half + 1) * HALF)
        gt_ref[:, cols] = (
            fin_send[c, :, cols].astype(F32) + fin_recv[:, cols].astype(F32)
        ).astype(BF)

    for copy in exchange + reduce + [final(0), final(1)]:
        copy.wait_send()

    def drain(k, carry):
        for h in range(2):
            send_unit(k, h).wait_send()
            fwd_y(k, h).wait_send()
        fwd_d1(k).wait_send()
        fwd_d2(k).wait_send()
        send_ra(k).wait_send()
        send_rb(k).wait_send()
        y_return(k).wait_send()
        send_home(k).wait_send()
        for j in range(4):
            xq_fwd(k, j).wait_send()
        for j in (1, 2, 3):
            xt_send(k, j).wait_send()
        return carry

    lax.fori_loop(0, NZ, drain, 0)
    for g in range(4):
        for j in (1, 2, 3):
            g_send(g, j).wait_send()


def on_device(tokens, grad_out, gates, routes, w_gate, w_up, w_down):
    dma = pltpu.SemaphoreType.DMA
    vmem = pl.BlockSpec(memory_space=pltpu.VMEM)
    anyspace = pl.BlockSpec(memory_space=pl.ANY)
    flops = 2 * 1536 * D * F * 7
    grad_tokens, grad_gate, grad_up, grad_down = pl.pallas_call(
        kernel,
        out_shape=(
            jax.ShapeDtypeStruct((T, D), BF),
            jax.ShapeDtypeStruct((QUART, F), BF),
            jax.ShapeDtypeStruct((QUART, F), BF),
            jax.ShapeDtypeStruct((F, QUART), BF),
        ),
        in_specs=[anyspace, anyspace, vmem, vmem, anyspace, anyspace, anyspace],
        out_specs=(vmem, vmem, vmem, vmem),
        scratch_shapes=[
            pltpu.VMEM((4 * T, D), BF),
            pltpu.VMEM((2, 8, T), F32),
            pltpu.VMEM((NZ, UNIT, D), BF),
            pltpu.VMEM((NZ, 4, UNIT, D), BF),
            pltpu.VMEM((D, F), BF),
            pltpu.VMEM((D, F), BF),
            pltpu.VMEM((F, D), BF),
            pltpu.VMEM((F, 32 * UNIT), BF),
            pltpu.VMEM((NZ, 4, UNIT, HALF), BF),
            pltpu.VMEM((NZ, UNIT, HALF), BF),
            pltpu.VMEM((NZ, UNIT, HALF), BF),
            pltpu.VMEM((NZ, UNIT, HALF), BF),
            pltpu.VMEM((NZ, UNIT, HALF), BF),
            pltpu.VMEM((4, F, QUART), BF),
            pltpu.VMEM((2, 128, QUART), BF),
            pltpu.VMEM((2, F, QUART), BF),
            pltpu.VMEM((2, T, D), BF),
            pltpu.VMEM((T, D), BF),
            pltpu.VMEM((2, 2 * T, NZ * UNIT), BF),
            pltpu.VMEM((NZ, UNIT, D), BF),
            pltpu.VMEM((4, 4, 2, 2, UNIT, QUART), BF),
            pltpu.VMEM((4, 4, 192, 2 * F), BF),
            pltpu.VMEM((2, F, QUART), F32),
            dma((5,)), dma((3,)), dma((3,)),
            dma((NZ, 2)), dma((NZ, 2)), dma((NZ, 2)), dma((NZ, 2)),
            dma((NZ,)), dma((NZ,)), dma((NZ,)), dma((NZ,)),
            dma((NZ,)), dma((NZ,)), dma((NZ,)), dma((NZ,)),
            dma((NZ,)), dma((NZ,)), dma((NZ,)), dma((NZ,)),
            dma((6,)), dma((6,)), dma((2,)), dma((2,)),
            dma((NZ, 4)), dma((NZ, 4)), dma((NZ, 4)), dma((NZ, 4)), dma((4, 4)), dma((4, 4)),
        ],
        compiler_params=pltpu.CompilerParams(
            collective_id=0, has_side_effects=True, vmem_limit_bytes=62 * 1024 * 1024
        ),
        cost_estimate=pl.CostEstimate(flops=flops, bytes_accessed=10_000_000, transcendentals=0),
    )(
        tokens, grad_out, gates.reshape(1, T), routes.reshape(1, T),
        w_gate[0], w_up[0], w_down[0],
    )
    return (grad_tokens, grad_gate[None], grad_up[None], grad_down[None])


def solution(mesh):
    in_specs = (
        P(("rep", "node", "local"), None),
        P(("rep", "node", "local"), None),
        P(("rep", "node", "local"), None),
        P(("rep", "node", "local"), None),
        P(("node", "local"), None, None),
        P(("node", "local"), None, None),
        P(("node", "local"), None, None),
    )
    out_specs = (
        P(("rep", "node", "local"), None),
        P(("node", "local"), "rep", None),
        P(("node", "local"), "rep", None),
        P(("node", "local"), None, "rep"),
    )
    return jax.shard_map(
        on_device, mesh=mesh, in_specs=in_specs, out_specs=out_specs, check_vma=False
    )
```
